32 devices in a mesh: parts: 2 (over y), ctx: 16 (over z, x, core).
Axes of the slice: x: 2, y: 2, z: 4, core: 2. Of those that a mesh axis runs over, the one named last changes fastest.
Arguments:
- tokens: bfloat16 [4096, 1024], P(('parts', 'ctx')), parts along dimension 0, may hold values from -8 to 8
- boundary: int32 [4096], P(('parts', 'ctx')), parts along dimension 0, may hold values from 0 to 1, as said below
- w_qkv_full: bfloat16 [1024, 1536], replicated, may hold values from -2 to 2
- w_out_full: bfloat16 [512, 1024], replicated, may hold values from -2 to 2
- w_qkv_short: bfloat16 [1024, 1536], replicated, may hold values from -2 to 2
- w_out_short: bfloat16 [512, 1024], replicated, may hold values from -1.5 to 1.5
Outputs:
- upsampled: bfloat16 [4096, 1024], P(('parts', 'ctx')), parts along dimension 0
The draws below stay inside these ranges and needn't reach their ends.
There are 2 independent parts, one for each index of `parts`. The reference program is written for one: setup_inputs(seed, part) draws one part's arguments, and reference() takes and returns one part's arrays. A program takes and returns all parts, laid end to end along the dimension named above; an argument that names none is the same for every part. Nothing has to cross between parts.
Inputs may be any that keep to these rules, and one draw needn't show every extreme that they name: `boundary`: the first token of the sequence is marked. The tokens of one device hold 16, 32 or 64 marks; in each aligned group of four devices these counts are 64, 32, 16, 16 in some order, so that all marks together number 512. The marks in the tokens of devices 0 to d - 1 number between (d - 1) * 32 and (d + 1) * 32; both bounds and the count 64 are reached in every draw.
All inputs are finite; a program needn't handle non-finite values.
Results may differ from the reference program's by a relative error of at most 0.012.
The reference program's roundings to bfloat16 on the way count: a program that leaves them out, or rounds other values in their place, can miss the bound.
Values may be sent and summed in bfloat16 or wider, within the bound.
A program may use at most 128 MiB of HBM per device.

```python
import jax
import jax.numpy as jnp
from jax import lax

D = 1024
HEADS = 8
HEAD_DIM = 64
TOK_DEV = 128
INNER = 512
WINDOW = 128
SHORT_DEV = 32
TOKENS = 2048
SHORT = 512
N_CTX = 16


def draw_tokens(key, part):
    key = jax.random.fold_in(key, 11)
    key_rows = jax.random.fold_in(key, 0)
    normal_draw = jnp.clip(jax.random.normal(key_rows, (TOKENS, D), jnp.float32), -6.0, 6.0)
    return normal_draw.astype(jnp.bfloat16)


def untied_weights(key):
    return jnp.clip(jax.random.normal(key, (D, 3 * INNER), jnp.float32), -4.0, 4.0) * D ** (-0.5)


def draw_w_qkv_full(key, part):
    key = jax.random.fold_in(key, 23)
    untied = untied_weights(key)
    return untied.astype(jnp.bfloat16)


def draw_w_qkv_short(key, part):
    key = jax.random.fold_in(key, 37)
    untied = untied_weights(key)
    return untied.astype(jnp.bfloat16)


def draw_boundary(key, part):
    key = jax.random.fold_in(key, 5)
    key_order, key_marks = jax.random.split(key)
    blocks = TOKENS // TOK_DEV
    groups = blocks // 4
    pattern = jnp.array([2 * SHORT_DEV, SHORT_DEV // 2, SHORT_DEV, SHORT_DEV // 2], jnp.int32)
    order_scores = jax.random.randint(key_order, (groups, 4), 0, 1 << 20) * 4 + jnp.arange(4, dtype=jnp.int32)[None, :]
    order_scores = order_scores.at[0, 0].set(-4)
    order_scores = order_scores.at[1, 1].set(-3).at[1, 3].set(-2)
    device_order = jnp.argsort(order_scores, axis=1)
    counts = pattern[device_order].reshape(blocks)
    position_scores = jax.random.randint(key_marks, (blocks, TOK_DEV), 0, 1 << 20) * TOK_DEV + jnp.arange(TOK_DEV, dtype=jnp.int32)[None, :]
    position_scores = position_scores.at[0, 0].set(-1)
    position_rank = jnp.argsort(jnp.argsort(position_scores, axis=1), axis=1)
    marks = (position_rank < counts[:, None]).astype(jnp.int32)
    return marks.reshape(TOKENS)


def scatter_about(key, extent, deviation, limit, held_as=jnp.bfloat16):
    return jnp.clip(deviation * jax.random.normal(key, extent, jnp.float32), -limit, limit).astype(held_as)


def setup_inputs(seed: int = 0, part: int = 0) -> dict:
    seeds = jax.random.split(jax.random.key(seed), 7)
    part_keys = jax.random.split(jax.random.fold_in(seeds[6], part), 7)
    tokens = draw_tokens(jax.random.fold_in(jax.random.fold_in(seeds[6], part), 71), part)
    boundary = draw_boundary(jax.random.fold_in(jax.random.fold_in(seeds[6], part), 71), part)
    w_qkv_full = draw_w_qkv_full(jax.random.fold_in(seeds[6], 71), part)
    w_out_full = scatter_about(seeds[3], (INNER, D), 0.15, 2.0)
    w_qkv_short = draw_w_qkv_short(jax.random.fold_in(seeds[6], 71), part)
    w_out_short = scatter_about(seeds[5], (INNER, D), 0.1, 1.5)
    return dict(tokens=tokens, boundary=boundary, w_qkv_full=w_qkv_full, w_out_full=w_out_full, w_qkv_short=w_qkv_short, w_out_short=w_out_short)


EPSILON = 1e-06
MASKED = -1e+30

def normalize(matrix):
    values = matrix.astype(jnp.float32)
    inverse = lax.rsqrt(lax.optimization_barrier(jnp.mean(values * values, axis=-1, keepdims=True)) + EPSILON)
    return (values * inverse).astype(jnp.bfloat16)

def split_heads(columns):
    return columns.reshape(columns.shape[0], HEADS, HEAD_DIM).transpose(1, 0, 2)

def attend(queries, key_block, value_block, allowed):
    query_heads = split_heads(queries).astype(jnp.float32)
    key_heads = split_heads(key_block).astype(jnp.float32)
    value_heads = split_heads(value_block).astype(jnp.float32)
    scores = jnp.einsum('hqd,hkd->hqk', query_heads, key_heads) * HEAD_DIM ** (-0.5)
    scores = jnp.where(allowed[None], scores, MASKED)
    highest = lax.optimization_barrier(jnp.max(scores, axis=-1, keepdims=True))
    expsum = jnp.where(allowed[None], jnp.exp(scores - highest), 0.0)
    row_total = lax.optimization_barrier(jnp.sum(expsum, axis=-1, keepdims=True))
    rounded = lax.optimization_barrier(expsum.astype(jnp.bfloat16)).astype(jnp.float32)
    mixed_heads = jnp.einsum('hqk,hkd->hqd', rounded, value_heads) / row_total
    return mixed_heads.transpose(1, 0, 2).reshape(queries.shape[0], HEADS * HEAD_DIM).astype(jnp.bfloat16)

def reference(tokens, boundary, w_qkv_full, w_out_full, w_qkv_short, w_out_short):
    inner_width = HEADS * HEAD_DIM
    segment = (jnp.cumsum(boundary) - 1).astype(jnp.int32)
    normed = normalize(tokens)
    packed = jnp.dot(normed, w_qkv_full, preferred_element_type=jnp.float32).astype(jnp.bfloat16)
    padded = jnp.concatenate([jnp.zeros((TOK_DEV, 3 * inner_width), jnp.bfloat16), packed], axis=0)
    offsets = jnp.arange(TOK_DEV, dtype=jnp.int32)
    key_offsets = jnp.arange(2 * TOK_DEV, dtype=jnp.int32)

    def window_block(block_index):
        block_start = (block_index * TOK_DEV).astype(jnp.int32)
        local_rows = lax.dynamic_slice_in_dim(packed, block_start, TOK_DEV, 0)
        beside_all = lax.dynamic_slice_in_dim(padded, block_start, 2 * TOK_DEV, 0)
        query_pos = block_start + offsets
        key_pos = block_start - TOK_DEV + key_offsets
        allowed = (key_pos[None, :] <= query_pos[:, None]) & (key_pos[None, :] > query_pos[:, None] - WINDOW) & (key_pos[None, :] >= 0)
        return attend(local_rows[:, :inner_width], beside_all[:, inner_width:2 * inner_width], beside_all[:, 2 * inner_width:], allowed)
    mixed_full = lax.map(window_block, jnp.arange(N_CTX, dtype=jnp.int32)).reshape(TOKENS, inner_width)
    stream = (tokens.astype(jnp.float32) + jnp.dot(mixed_full, w_out_full, preferred_element_type=jnp.float32)).astype(jnp.bfloat16)
    seg_sums = jax.ops.segment_sum(stream.astype(jnp.float32), segment, num_segments=SHORT)
    seg_sizes = jax.ops.segment_sum(jnp.ones((TOKENS,), jnp.float32), segment, num_segments=SHORT)
    pooled = (seg_sums / seg_sizes[:, None]).astype(jnp.bfloat16)
    short_packed = jnp.dot(normalize(pooled), w_qkv_short, preferred_element_type=jnp.float32).astype(jnp.bfloat16)
    short_rows = jnp.arange(SHORT, dtype=jnp.int32)
    short_offsets = jnp.arange(SHORT_DEV, dtype=jnp.int32)

    def causal_block(block_index):
        block_start = (block_index * SHORT_DEV).astype(jnp.int32)
        local_rows = lax.dynamic_slice_in_dim(short_packed, block_start, SHORT_DEV, 0)
        query_pos = block_start + short_offsets
        allowed = short_rows[None, :] <= query_pos[:, None]
        return attend(local_rows[:, :inner_width], short_packed[:, inner_width:2 * inner_width], short_packed[:, 2 * inner_width:], allowed)
    mixed_short = lax.map(causal_block, jnp.arange(N_CTX, dtype=jnp.int32)).reshape(SHORT, inner_width)
    short_out = (pooled.astype(jnp.float32) + jnp.dot(mixed_short, w_out_short, preferred_element_type=jnp.float32)).astype(jnp.bfloat16)
    shifted_out = jnp.concatenate([jnp.zeros((1, D), jnp.bfloat16), short_out[:-1]], axis=0)
    return (stream.astype(jnp.float32) + shifted_out[segment].astype(jnp.float32)).astype(jnp.bfloat16)
```

```python
import functools

import jax
import jax.numpy as jnp
from jax import lax
from jax.experimental import pallas as pl
from jax.experimental.pallas import tpu as pltpu
from jax.sharding import PartitionSpec as P

HEADS = 8
HEAD_DIM = 64
WINDOW = 128
INNER = HEADS * HEAD_DIM
PAIR = 2 * HEAD_DIM
GROUP = 4
TAIL = 16
EPSILON = 1e-06
MASKED = -1e30
SCALE = HEAD_DIM ** (-0.5)
F32 = jnp.float32
BF16 = jnp.bfloat16
NT = (((1,), (1,)), ((), ()))


def normalize(matrix):
    values = matrix.astype(F32)
    inverse = lax.rsqrt(jnp.mean(values * values, axis=-1, keepdims=True) + EPSILON)
    return (values * inverse).astype(BF16)


def dot(a, b):
    return jnp.dot(a, b, preferred_element_type=F32)


def iota(shape, dim):
    return lax.broadcasted_iota(jnp.int32, shape, dim)


def onehot(condition):
    return jnp.where(condition, 1.0, 0.0).astype(BF16)


def stack_heads(q_pair):
    low = iota(q_pair.shape, 1) < HEAD_DIM
    zero = jnp.zeros_like(q_pair)
    return jnp.concatenate([jnp.where(low, q_pair, zero), jnp.where(low, zero, q_pair)], axis=0)


def unstack_heads(stacked):
    rows = stacked.shape[0] // 2
    low = iota((rows, PAIR), 1) < HEAD_DIM
    return jnp.where(low, stacked[:rows], stacked[rows:])


def kernel(
    n, tokens, boundary, wqf_hbm, wof_hbm, wqs_hbm, wos_hbm, out,
    wqf, wof, wqs, wos, prev, kv_cat, lead_out, lead_in, marks, parted, joined, rows_out, rows_in,
    kv_all, mix, mix_tail,
    w_sem, tok_s, tok_r, lead_s, lead_r, marks_s, marks_r, part_s, part_r, rows_s, rows_r,
    kv_s, kv_r, mix_s, mix_r, mt_s, mt_r,
):
    length, width = tokens.shape
    capacity = length // 2
    groups = n // GROUP
    me = lax.axis_index("ctx")
    group = me // GROUP
    lane = lax.rem(me, GROUP)

    def remote(src, dst, s_sem, r_sem, device):
        return pltpu.make_async_remote_copy(
            src_ref=src, dst_ref=dst, send_sem=s_sem, recv_sem=r_sem,
            device_id={"ctx": device}, device_id_type=pl.DeviceIdType.MESH,
        )

    weights = [
        pltpu.make_async_copy(src, dst, w_sem.at[i])
        for i, (src, dst) in enumerate([(wqf_hbm, wqf), (wof_hbm, wof), (wqs_hbm, wqs), (wos_hbm, wos)])
    ]

    barrier = pltpu.get_barrier_semaphore()

    def greet(k, carry):
        pl.semaphore_signal(
            barrier, inc=1, device_id={"ctx": lax.rem(me + k, n)}, device_id_type=pl.DeviceIdType.MESH
        )
        return carry

    lax.fori_loop(1, n, greet, 0)
    for copy in weights:
        copy.start()

    after = lax.rem(me + 1, n)
    before = lax.rem(me + n - 1, n)
    peers = [lax.rem(lane + k, GROUP) for k in range(1, GROUP)]
    bound = boundary[...]
    marks[lane] = jnp.broadcast_to(bound, (8, length))

    @pl.when(me == 0)
    def _():
        prev[...] = jnp.zeros_like(prev)
        rows_in[...] = jnp.zeros_like(rows_in)

    @pl.when(me == n - 1)
    def _():
        lead_in[...] = jnp.zeros_like(lead_in)

    @pl.when((lane != 0) | (group == 0))
    def _():
        mix_tail[...] = jnp.zeros_like(mix_tail)

    pl.semaphore_wait(barrier, n - 1)

    tok_copy = remote(tokens, prev, tok_s, tok_r, after)

    @pl.when(me < n - 1)
    def _():
        tok_copy.start()

    marks_copies = [
        remote(marks.at[lane], marks.at[lane], marks_s.at[k], marks_r.at[lane], group * GROUP + peer)
        for k, peer in enumerate(peers)
    ]
    for copy in marks_copies:
        copy.start()

    tok = tokens[...]
    normed = normalize(tok)
    weights[0].wait()
    packed = dot(normed, wqf[...]).astype(BF16)
    queries = packed[:, :INNER]
    kv_cat[length:, :] = packed[:, INNER:]

    bound_rows = jnp.broadcast_to(bound.astype(F32), (length, length)).astype(BF16)
    i0 = iota((length, length), 0)
    i1 = iota((length, length), 1)
    seg_lane = dot(bound_rows, onehot(i0 <= i1)).astype(jnp.int32) - 1
    seg_sub = lax.dot_general(onehot(i1 <= i0), bound_rows, NT, preferred_element_type=F32).astype(jnp.int32) - 1
    starts = jnp.sum(bound, axis=1, keepdims=True)

    @pl.when(me > 0)
    def _():
        remote(tokens, prev, tok_s, tok_r, before).wait_recv()

    kv_cat[:length, :] = dot(normalize(prev[...]), wqf[:, INNER:]).astype(BF16)

    q_pos = iota((length, 2 * length), 0) + length
    k_pos = iota((length, 2 * length), 1)
    first_key = jnp.where(me == 0, length, 0)
    allowed = (k_pos <= q_pos) & (k_pos > q_pos - WINDOW) & (k_pos >= first_key)
    allowed = jnp.concatenate([allowed, allowed], axis=0)
    mixed = []
    for p in range(HEADS // 2):
        cols = slice(p * PAIR, (p + 1) * PAIR)
        scores = lax.dot_general(stack_heads(queries[:, cols]), kv_cat[:, cols], NT, preferred_element_type=F32)
        scores = jnp.where(allowed, scores, MASKED)
        highest = jnp.max(scores, axis=-1, keepdims=True)
        expsum = jnp.exp((scores - highest) * SCALE)
        total = jnp.sum(expsum, axis=-1, keepdims=True)
        values = kv_cat[:, INNER + p * PAIR:INNER + (p + 1) * PAIR]
        mixed.append(unstack_heads(dot(expsum.astype(BF16), values) / total).astype(BF16))
    weights[1].wait()
    stream = (tok.astype(F32) + dot(jnp.concatenate(mixed, axis=1), wof[...])).astype(BF16)

    slots = capacity + TAIL
    slot = iota((slots, length), 0)
    gather = onehot(jnp.where(slot == capacity, -1, slot) == seg_lane[:slots])
    partial = dot(gather, stream)
    sizes = jnp.sum(gather.astype(F32), axis=1, keepdims=True)
    lead_out[:, :width] = partial[capacity:capacity + 8]
    lead_out[:, width:] = jnp.broadcast_to(sizes[capacity:capacity + 8], (8, 128))
    lead_copy = remote(lead_out, lead_in, lead_s, lead_r, before)

    @pl.when(me > 0)
    def _():
        lead_copy.start()

    slot_col = iota((capacity, 1), 0)
    closing = jnp.where(slot_col == starts - 1, 1.0, 0.0)
    weights[2].wait()

    @pl.when(me < n - 1)
    def _():
        remote(lead_out, lead_in, lead_s, lead_r, after).wait_recv()

    lead = lead_in[0:1, :]
    totals = partial[:capacity] + closing * lead[:, :width]
    seg_sizes = sizes[:capacity] + closing * lead[:, width:width + 1]
    pooled = (totals / jnp.maximum(seg_sizes, 1.0)).astype(BF16)

    short = dot(normalize(pooled), wqs[...]).astype(BF16)
    for j in range(GROUP):
        for part in range(3):
            parted[j, :, part * PAIR:(part + 1) * PAIR] = short[:, part * INNER + j * PAIR:part * INNER + (j + 1) * PAIR]
    part_copies = [
        remote(parted.at[peer], joined.at[lane], part_s.at[k], part_r.at[lane], group * GROUP + peer)
        for k, peer in enumerate(peers)
    ]
    for copy in part_copies:
        copy.start()
    joined[lane] = parted[lane]

    tail_row = iota((TAIL, capacity), 0)
    tail_slot = iota((TAIL, capacity), 1)
    rows_out[...] = dot(onehot((tail_row < 2) & (tail_slot == starts - 1 - tail_row)), pooled).astype(BF16)
    rows_copy = remote(rows_out, rows_in, rows_s, rows_r, after)

    @pl.when(me < n - 1)
    def _():
        rows_copy.start()

    for k, peer in enumerate(peers):
        remote(marks.at[lane], marks.at[peer], marks_s.at[k], marks_r.at[peer], group * GROUP + peer).wait_recv()
    counts = [jnp.sum(marks[j][0:1], axis=1, keepdims=True) for j in range(GROUP)]
    firsts = [jnp.zeros_like(counts[0])]
    for j in range(GROUP - 1):
        firsts.append(firsts[-1] + counts[j])
    my_first = firsts[0]
    for j in range(1, GROUP):
        my_first = jnp.where(lane == j, firsts[j], my_first)

    place = iota((length, GROUP * capacity), 0)
    source = iota((length, GROUP * capacity), 1)
    owner_first = jnp.broadcast_to(firsts[0], place.shape)
    owner_count = jnp.broadcast_to(counts[0], place.shape)
    for j in range(1, GROUP):
        beyond = source >= j * capacity
        owner_first = jnp.where(beyond, firsts[j], owner_first)
        owner_count = jnp.where(beyond, counts[j], owner_count)
    within = source & (capacity - 1)
    compact = onehot((within < owner_count) & (within + owner_first == place))

    for k, peer in enumerate(peers):
        remote(parted.at[lane], joined.at[peer], part_s.at[k], part_r.at[peer], group * GROUP + peer).wait_recv()
    rows = dot(compact, joined[...].reshape(GROUP * capacity, 3 * PAIR)).astype(BF16)
    kv_all[group] = rows[:, PAIR:]

    def kv_copy(other):
        return remote(kv_all.at[group], kv_all.at[group], kv_s.at[other], kv_r.at[group], other * GROUP + lane)

    def send(other, carry):
        kv_copy(other).start()
        return carry

    lax.fori_loop(group + 1, groups, send, 0)

    q_stack = stack_heads(rows[:, :PAIR])
    scores = lax.dot_general(q_stack, rows[:, PAIR:2 * PAIR], NT, preferred_element_type=F32)
    causal = i1 <= i0
    scores = jnp.where(jnp.concatenate([causal, causal], axis=0), scores, MASKED)
    row_max = jnp.max(scores, axis=-1, keepdims=True)
    expsum = jnp.exp((scores - row_max) * SCALE)
    row_total = jnp.sum(expsum, axis=-1, keepdims=True)
    running = dot(expsum.astype(BF16), rows[:, 2 * PAIR:])

    @pl.when(me > 0)
    def _():
        remote(rows_out, rows_in, rows_s, rows_r, before).wait_recv()

    lift = onehot(iota((length, capacity), 1) == seg_sub[:, :capacity] - 1)
    lift_tail = onehot(iota((length, TAIL), 1) == -seg_sub[:, :TAIL])
    pooled_lifted = dot(lift, pooled) + dot(lift_tail, rows_in[...])

    def attend(step, carry):
        row_max, row_total, running = carry
        other = group - 1 - step
        remote(
            kv_all.at[other], kv_all.at[other], kv_s.at[other], kv_r.at[other], other * GROUP + lane
        ).wait_recv()
        block = kv_all[other]
        scores = lax.dot_general(q_stack, block[:, :PAIR], NT, preferred_element_type=F32)
        new_max = jnp.maximum(row_max, jnp.max(scores, axis=-1, keepdims=True))
        expsum = jnp.exp((scores - new_max) * SCALE)
        fading = jnp.exp((row_max - new_max) * SCALE)
        row_total = row_total * fading + jnp.sum(expsum, axis=-1, keepdims=True)
        running = running * fading + dot(expsum.astype(BF16), block[:, PAIR:])
        return new_max, row_total, running

    row_max, row_total, running = lax.fori_loop(0, group, attend, (row_max, row_total, running))
    mix[lane] = unstack_heads(running / row_total).astype(BF16)

    mix_copies = [
        remote(mix.at[lane], mix.at[lane], mix_s.at[k], mix_r.at[lane], group * GROUP + peer)
        for k, peer in enumerate(peers)
    ]
    for copy in mix_copies:
        copy.start()
    next_lead = lax.rem((group + 1) * GROUP, n)
    mt_copy = remote(
        mix.at[lane, pl.ds(length - TAIL, TAIL)], mix_tail.at[lane], mt_s, mt_r.at[lane], next_lead
    )

    @pl.when(group < groups - 1)
    def _():
        mt_copy.start()

    weights[3].wait()
    target = seg_sub + my_first - 1
    pick = onehot(i1 == target)
    pick_tail = onehot(iota((length, TAIL), 1) == target[:, :TAIL] + TAIL)
    for k, peer in enumerate(peers):
        remote(mix.at[peer], mix.at[peer], mix_s.at[k], mix_r.at[peer], group * GROUP + peer).wait_recv()

    @pl.when((lane == 0) & (group > 0))
    def _():
        for j in range(GROUP):
            remote(
                mix.at[j, pl.ds(length - TAIL, TAIL)], mix_tail.at[j], mt_s, mt_r.at[j], before
            ).wait_recv()

    mixed_rows = jnp.concatenate([mix[j] for j in range(GROUP)], axis=1)
    tail_rows = jnp.concatenate([mix_tail[j] for j in range(GROUP)], axis=1)
    lifted = (dot(pick, mixed_rows) + dot(pick_tail, tail_rows)).astype(BF16)
    short_out = (pooled_lifted + dot(lifted, wos[...])).astype(BF16)
    out[...] = (stream.astype(F32) + short_out.astype(F32)).astype(BF16)

    @pl.when(me < n - 1)
    def _():
        tok_copy.wait_send()
        rows_copy.wait_send()

    @pl.when(me > 0)
    def _():
        lead_copy.wait_send()

    for copy in marks_copies + part_copies + mix_copies:
        copy.wait_send()

    def drain(other, carry):
        kv_copy(other).wait_send()
        return carry

    lax.fori_loop(group + 1, groups, drain, 0)

    @pl.when(group < groups - 1)
    def _():
        mt_copy.wait_send()


def shards(n, tokens, boundary, w_qkv_full, w_out_full, w_qkv_short, w_out_short):
    length, width = tokens.shape
    capacity = length // 2
    groups = n // GROUP
    vmem = pl.BlockSpec(memory_space=pltpu.VMEM)
    hbm = pl.BlockSpec(memory_space=pl.ANY)
    dma = pltpu.SemaphoreType.DMA
    return pl.pallas_call(
        functools.partial(kernel, n),
        out_shape=jax.ShapeDtypeStruct((length, width), BF16),
        in_specs=[vmem, vmem, hbm, hbm, hbm, hbm],
        out_specs=vmem,
        scratch_shapes=[
            pltpu.VMEM(w_qkv_full.shape, BF16),
            pltpu.VMEM(w_out_full.shape, BF16),
            pltpu.VMEM(w_qkv_short.shape, BF16),
            pltpu.VMEM(w_out_short.shape, BF16),
            pltpu.VMEM((length, width), BF16),
            pltpu.VMEM((2 * length, 2 * INNER), BF16),
            pltpu.VMEM((8, width + 128), F32),
            pltpu.VMEM((8, width + 128), F32),
            pltpu.VMEM((GROUP, 8, length), jnp.int32),
            pltpu.VMEM((GROUP, capacity, 3 * PAIR), BF16),
            pltpu.VMEM((GROUP, capacity, 3 * PAIR), BF16),
            pltpu.VMEM((TAIL, width), BF16),
            pltpu.VMEM((TAIL, width), BF16),
            pltpu.VMEM((groups, length, 2 * PAIR), BF16),
            pltpu.VMEM((GROUP, length, PAIR), BF16),
            pltpu.VMEM((GROUP, TAIL, PAIR), BF16),
            dma((4,)),
            dma, dma, dma, dma,
            dma((GROUP,)), dma((GROUP,)),
            dma((GROUP,)), dma((GROUP,)),
            dma, dma,
            dma((groups,)), dma((groups,)),
            dma((GROUP,)), dma((GROUP,)),
            dma, dma((GROUP,)),
        ],
        compiler_params=pltpu.CompilerParams(
            collective_id=0, has_side_effects=True, vmem_limit_bytes=40 * 1024 * 1024
        ),
    )(tokens, boundary.reshape(1, length), w_qkv_full, w_out_full, w_qkv_short, w_out_short)


def solution(mesh):
    return jax.shard_map(
        functools.partial(shards, mesh.shape["ctx"]),
        mesh=mesh,
        in_specs=(P(("parts", "ctx"), None), P(("parts", "ctx")), P(), P(), P(), P()),
        out_specs=P(("parts", "ctx"), None),
        check_vma=False,
    )
```

```python
import functools

import jax
import jax.numpy as jnp
from jax import lax
from jax.experimental import pallas as pl
from jax.experimental.pallas import tpu as pltpu
from jax.sharding import PartitionSpec as P

HEADS = 8
HEAD_DIM = 64
WINDOW = 128
INNER = HEADS * HEAD_DIM
PAIR = 2 * HEAD_DIM
GROUP = 4
TAIL = 16
EPSILON = 1e-06
MASKED = -1e30
SCALE = HEAD_DIM ** (-0.5)
F32 = jnp.float32
BF16 = jnp.bfloat16
NT = (((1,), (1,)), ((), ()))


def normalize(matrix):
    values = matrix.astype(F32)
    inverse = lax.rsqrt(jnp.mean(values * values, axis=-1, keepdims=True) + EPSILON)
    return (values * inverse).astype(BF16)


def dot(a, b):
    return jnp.dot(a, b, preferred_element_type=F32)


def iota(shape, dim):
    return lax.broadcasted_iota(jnp.int32, shape, dim)


def onehot(condition):
    return jnp.where(condition, 1.0, 0.0).astype(BF16)


def stack_heads(q_pair):
    low = iota(q_pair.shape, 1) < HEAD_DIM
    zero = jnp.zeros_like(q_pair)
    return jnp.concatenate([jnp.where(low, q_pair, zero), jnp.where(low, zero, q_pair)], axis=0)


def unstack_heads(stacked):
    rows = stacked.shape[0] // 2
    low = iota((rows, PAIR), 1) < HEAD_DIM
    return jnp.where(low, stacked[:rows], stacked[rows:])


def kernel(
    n, tokens_hbm, boundary_hbm, wqf_hbm, wof_hbm, wqs_hbm, wos_hbm, out,
    tokens, boundary, wqf, wof, wqs, wos, prev, kv_cat, lead_out, lead_in, marks, parted, joined, rows_out, rows_in,
    kv_all, mix, mix_tail,
    w_sem, tok_s, tok_r, lead_s, lead_r, marks_s, marks_r, part_s, part_r, rows_s, rows_r,
    kv_s, kv_r, mix_s, mix_r, mt_s, mt_r,
):
    length, width = tokens.shape
    capacity = length // 2
    groups = n // GROUP
    me = lax.axis_index("ctx")
    group = me // GROUP
    lane = lax.rem(me, GROUP)

    def remote(src, dst, s_sem, r_sem, device):
        return pltpu.make_async_remote_copy(
            src_ref=src, dst_ref=dst, send_sem=s_sem, recv_sem=r_sem,
            device_id={"ctx": device}, device_id_type=pl.DeviceIdType.MESH,
        )

    weights = [
        pltpu.make_async_copy(src, dst, w_sem.at[i])
        for i, (src, dst) in enumerate([
            (wqf_hbm, wqf), (wof_hbm, wof), (wqs_hbm, wqs), (wos_hbm, wos),
            (tokens_hbm, tokens), (boundary_hbm, boundary),
        ])
    ]

    barrier = pltpu.get_barrier_semaphore()

    def greet(k, carry):
        pl.semaphore_signal(
            barrier, inc=1, device_id={"ctx": lax.rem(me + k, n)}, device_id_type=pl.DeviceIdType.MESH
        )
        return carry

    lax.fori_loop(1, n, greet, 0)
    for i in (4, 5, 0, 1, 2, 3):
        weights[i].start()

    after = lax.rem(me + 1, n)
    before = lax.rem(me + n - 1, n)
    peers = [lax.rem(lane + k, GROUP) for k in range(1, GROUP)]
    weights[5].wait()
    bound = boundary[...]
    marks[lane] = jnp.broadcast_to(bound, (8, length))

    @pl.when(me == 0)
    def _():
        prev[...] = jnp.zeros_like(prev)
        rows_in[...] = jnp.zeros_like(rows_in)

    @pl.when(me == n - 1)
    def _():
        lead_in[...] = jnp.zeros_like(lead_in)

    @pl.when((lane != 0) | (group == 0))
    def _():
        mix_tail[...] = jnp.zeros_like(mix_tail)

    bound_rows = jnp.broadcast_to(bound.astype(F32), (length, length)).astype(BF16)
    i0 = iota((length, length), 0)
    i1 = iota((length, length), 1)
    seg_lane = dot(bound_rows, onehot(i0 <= i1)).astype(jnp.int32) - 1
    seg_sub = lax.dot_general(onehot(i1 <= i0), bound_rows, NT, preferred_element_type=F32).astype(jnp.int32) - 1
    starts = jnp.sum(bound, axis=1, keepdims=True)

    weights[4].wait()
    tok = tokens[...]
    normed = normalize(tok)
    pl.semaphore_wait(barrier, n - 1)

    tok_copy = remote(tokens_hbm, prev, tok_s, tok_r, after)

    @pl.when(me < n - 1)
    def _():
        tok_copy.start()

    marks_copies = [
        remote(marks.at[lane], marks.at[lane], marks_s.at[k], marks_r.at[lane], group * GROUP + peer)
        for k, peer in enumerate(peers)
    ]
    for copy in marks_copies:
        copy.start()

    weights[0].wait()
    packed = dot(normed, wqf[...]).astype(BF16)
    queries = packed[:, :INNER]
    kv_cat[length:, :] = packed[:, INNER:]

    @pl.when(me > 0)
    def _():
        remote(tokens_hbm, prev, tok_s, tok_r, before).wait_recv()

    kv_cat[:length, :] = dot(normalize(prev[...]), wqf[:, INNER:]).astype(BF16)

    q_pos = iota((length, 2 * length), 0) + length
    k_pos = iota((length, 2 * length), 1)
    first_key = jnp.where(me == 0, length, 0)
    allowed = (k_pos <= q_pos) & (k_pos > q_pos - WINDOW) & (k_pos >= first_key)
    allowed = jnp.concatenate([allowed, allowed], axis=0)
    mixed = []
    for p in range(HEADS // 2):
        cols = slice(p * PAIR, (p + 1) * PAIR)
        scores = lax.dot_general(stack_heads(queries[:, cols]), kv_cat[:, cols], NT, preferred_element_type=F32)
        scores = jnp.where(allowed, scores, MASKED)
        highest = jnp.max(scores, axis=-1, keepdims=True)
        expsum = jnp.exp((scores - highest) * SCALE)
        total = jnp.sum(expsum, axis=-1, keepdims=True)
        values = kv_cat[:, INNER + p * PAIR:INNER + (p + 1) * PAIR]
        mixed.append(unstack_heads(dot(expsum.astype(BF16), values) / total).astype(BF16))
    weights[1].wait()
    stream = (tok.astype(F32) + dot(jnp.concatenate(mixed, axis=1), wof[...])).astype(BF16)

    slots = capacity + TAIL
    slot = iota((slots, length), 0)
    gather = onehot(jnp.where(slot == capacity, -1, slot) == seg_lane[:slots])
    partial = dot(gather, stream)
    sizes = jnp.sum(gather.astype(F32), axis=1, keepdims=True)
    lead_out[:, :width] = partial[capacity:capacity + 8]
    lead_out[:, width:] = jnp.broadcast_to(sizes[capacity:capacity + 8], (8, 128))
    lead_copy = remote(lead_out, lead_in, lead_s, lead_r, before)

    @pl.when(me > 0)
    def _():
        lead_copy.start()

    slot_col = iota((capacity, 1), 0)
    closing = jnp.where(slot_col == starts - 1, 1.0, 0.0)
    weights[2].wait()

    @pl.when(me < n - 1)
    def _():
        remote(lead_out, lead_in, lead_s, lead_r, after).wait_recv()

    lead = lead_in[0:1, :]
    totals = partial[:capacity] + closing * lead[:, :width]
    seg_sizes = sizes[:capacity] + closing * lead[:, width:width + 1]
    pooled = (totals / jnp.maximum(seg_sizes, 1.0)).astype(BF16)

    short = dot(normalize(pooled), wqs[...]).astype(BF16)
    for j in range(GROUP):
        for part in range(3):
            parted[j, :, part * PAIR:(part + 1) * PAIR] = short[:, part * INNER + j * PAIR:part * INNER + (j + 1) * PAIR]
    part_copies = [
        remote(parted.at[peer], joined.at[lane], part_s.at[k], part_r.at[lane], group * GROUP + peer)
        for k, peer in enumerate(peers)
    ]
    for copy in part_copies:
        copy.start()
    joined[lane] = parted[lane]

    tail_row = iota((TAIL, capacity), 0)
    tail_slot = iota((TAIL, capacity), 1)
    rows_out[...] = dot(onehot((tail_row < 2) & (tail_slot == starts - 1 - tail_row)), pooled).astype(BF16)
    rows_copy = remote(rows_out, rows_in, rows_s, rows_r, after)

    @pl.when(me < n - 1)
    def _():
        rows_copy.start()

    for k, peer in enumerate(peers):
        remote(marks.at[lane], marks.at[peer], marks_s.at[k], marks_r.at[peer], group * GROUP + peer).wait_recv()
    counts = [jnp.sum(marks[j][0:1], axis=1, keepdims=True) for j in range(GROUP)]
    firsts = [jnp.zeros_like(counts[0])]
    for j in range(GROUP - 1):
        firsts.append(firsts[-1] + counts[j])
    my_first = firsts[0]
    for j in range(1, GROUP):
        my_first = jnp.where(lane == j, firsts[j], my_first)

    place = iota((length, GROUP * capacity), 0)
    source = iota((length, GROUP * capacity), 1)
    owner_first = jnp.broadcast_to(firsts[0], place.shape)
    owner_count = jnp.broadcast_to(counts[0], place.shape)
    for j in range(1, GROUP):
        beyond = source >= j * capacity
        owner_first = jnp.where(beyond, firsts[j], owner_first)
        owner_count = jnp.where(beyond, counts[j], owner_count)
    within = source & (capacity - 1)
    compact = onehot((within < owner_count) & (within + owner_first == place))

    for k, peer in enumerate(peers):
        remote(parted.at[lane], joined.at[peer], part_s.at[k], part_r.at[peer], group * GROUP + peer).wait_recv()
    rows = dot(compact, joined[...].reshape(GROUP * capacity, 3 * PAIR)).astype(BF16)
    kv_all[group] = rows[:, PAIR:]

    def kv_copy(other):
        return remote(kv_all.at[group], kv_all.at[group], kv_s.at[other], kv_r.at[group], other * GROUP + lane)

    def send(other, carry):
        kv_copy(other).start()
        return carry

    lax.fori_loop(group + 1, groups, send, 0)

    q_stack = stack_heads(rows[:, :PAIR])
    scores = lax.dot_general(q_stack, rows[:, PAIR:2 * PAIR], NT, preferred_element_type=F32)
    causal = i1 <= i0
    scores = jnp.where(jnp.concatenate([causal, causal], axis=0), scores, MASKED)
    row_max = jnp.max(scores, axis=-1, keepdims=True)
    expsum = jnp.exp((scores - row_max) * SCALE)
    row_total = jnp.sum(expsum, axis=-1, keepdims=True)
    running = dot(expsum.astype(BF16), rows[:, 2 * PAIR:])

    @pl.when(me > 0)
    def _():
        remote(rows_out, rows_in, rows_s, rows_r, before).wait_recv()

    lift = onehot(iota((length, capacity), 1) == seg_sub[:, :capacity] - 1)
    lift_tail = onehot(iota((length, TAIL), 1) == -seg_sub[:, :TAIL])
    pooled_lifted = dot(lift, pooled) + dot(lift_tail, rows_in[...])

    def attend(step, carry):
        row_max, row_total, running = carry
        other = group - 1 - step
        remote(
            kv_all.at[other], kv_all.at[other], kv_s.at[other], kv_r.at[other], other * GROUP + lane
        ).wait_recv()
        block = kv_all[other]
        scores = lax.dot_general(q_stack, block[:, :PAIR], NT, preferred_element_type=F32)
        new_max = jnp.maximum(row_max, jnp.max(scores, axis=-1, keepdims=True))
        expsum = jnp.exp((scores - new_max) * SCALE)
        fading = jnp.exp((row_max - new_max) * SCALE)
        row_total = row_total * fading + jnp.sum(expsum, axis=-1, keepdims=True)
        running = running * fading + dot(expsum.astype(BF16), block[:, PAIR:])
        return new_max, row_total, running

    row_max, row_total, running = lax.fori_loop(0, group, attend, (row_max, row_total, running))
    mix[lane] = unstack_heads(running / row_total).astype(BF16)

    mix_copies = [
        remote(mix.at[lane], mix.at[lane], mix_s.at[k], mix_r.at[lane], group * GROUP + peer)
        for k, peer in enumerate(peers)
    ]
    for copy in mix_copies:
        copy.start()
    next_lead = lax.rem((group + 1) * GROUP, n)
    mt_copy = remote(
        mix.at[lane, pl.ds(length - TAIL, TAIL)], mix_tail.at[lane], mt_s, mt_r.at[lane], next_lead
    )

    @pl.when(group < groups - 1)
    def _():
        mt_copy.start()

    weights[3].wait()
    target = seg_sub + my_first - 1
    pick = onehot(i1 == target)
    pick_tail = onehot(iota((length, TAIL), 1) == target[:, :TAIL] + TAIL)
    for k, peer in enumerate(peers):
        remote(mix.at[peer], mix.at[peer], mix_s.at[k], mix_r.at[peer], group * GROUP + peer).wait_recv()

    @pl.when((lane == 0) & (group > 0))
    def _():
        for j in range(GROUP):
            remote(
                mix.at[j, pl.ds(length - TAIL, TAIL)], mix_tail.at[j], mt_s, mt_r.at[j], before
            ).wait_recv()

    mixed_rows = jnp.concatenate([mix[j] for j in range(GROUP)], axis=1)
    tail_rows = jnp.concatenate([mix_tail[j] for j in range(GROUP)], axis=1)
    lifted = (dot(pick, mixed_rows) + dot(pick_tail, tail_rows)).astype(BF16)
    short_out = (pooled_lifted + dot(lifted, wos[...])).astype(BF16)
    out[...] = (stream.astype(F32) + short_out.astype(F32)).astype(BF16)

    @pl.when(me < n - 1)
    def _():
        tok_copy.wait_send()
        rows_copy.wait_send()

    @pl.when(me > 0)
    def _():
        lead_copy.wait_send()

    for copy in marks_copies + part_copies + mix_copies:
        copy.wait_send()

    def drain(other, carry):
        kv_copy(other).wait_send()
        return carry

    lax.fori_loop(group + 1, groups, drain, 0)

    @pl.when(group < groups - 1)
    def _():
        mt_copy.wait_send()


def shards(n, tokens, boundary, w_qkv_full, w_out_full, w_qkv_short, w_out_short):
    length, width = tokens.shape
    capacity = length // 2
    groups = n // GROUP
    vmem = pl.BlockSpec(memory_space=pltpu.VMEM)
    hbm = pl.BlockSpec(memory_space=pl.ANY)
    dma = pltpu.SemaphoreType.DMA
    return pl.pallas_call(
        functools.partial(kernel, n),
        out_shape=jax.ShapeDtypeStruct((length, width), BF16),
        in_specs=[hbm, hbm, hbm, hbm, hbm, hbm],
        out_specs=vmem,
        scratch_shapes=[
            pltpu.VMEM((length, width), BF16),
            pltpu.VMEM((1, length), jnp.int32),
            pltpu.VMEM(w_qkv_full.shape, BF16),
            pltpu.VMEM(w_out_full.shape, BF16),
            pltpu.VMEM(w_qkv_short.shape, BF16),
            pltpu.VMEM(w_out_short.shape, BF16),
            pltpu.VMEM((length, width), BF16),
            pltpu.VMEM((2 * length, 2 * INNER), BF16),
            pltpu.VMEM((8, width + 128), F32),
            pltpu.VMEM((8, width + 128), F32),
            pltpu.VMEM((GROUP, 8, length), jnp.int32),
            pltpu.VMEM((GROUP, capacity, 3 * PAIR), BF16),
            pltpu.VMEM((GROUP, capacity, 3 * PAIR), BF16),
            pltpu.VMEM((TAIL, width), BF16),
            pltpu.VMEM((TAIL, width), BF16),
            pltpu.VMEM((groups, length, 2 * PAIR), BF16),
            pltpu.VMEM((GROUP, length, PAIR), BF16),
            pltpu.VMEM((GROUP, TAIL, PAIR), BF16),
            dma((6,)),
            dma, dma, dma, dma,
            dma((GROUP,)), dma((GROUP,)),
            dma((GROUP,)), dma((GROUP,)),
            dma, dma,
            dma((groups,)), dma((groups,)),
            dma((GROUP,)), dma((GROUP,)),
            dma, dma((GROUP,)),
        ],
        compiler_params=pltpu.CompilerParams(
            collective_id=0, has_side_effects=True, vmem_limit_bytes=60 * 1024 * 1024
        ),
    )(tokens, boundary.reshape(1, length), w_qkv_full, w_out_full, w_qkv_short, w_out_short)


def solution(mesh):
    return jax.shard_map(
        functools.partial(shards, mesh.shape["ctx"]),
        mesh=mesh,
        in_specs=(P(("parts", "ctx"), None), P(("parts", "ctx")), P(), P(), P(), P()),
        out_specs=P(("parts", "ctx"), None),
        check_vma=False,
    )
```

```python
import functools

import jax
import jax.numpy as jnp
from jax import lax
from jax.experimental import pallas as pl
from jax.experimental.pallas import tpu as pltpu
from jax.sharding import PartitionSpec as P

HEADS = 8
HEAD_DIM = 64
WINDOW = 128
INNER = HEADS * HEAD_DIM
PAIR = 2 * HEAD_DIM
GROUP = 4
TAIL = 16
EPSILON = 1e-06
MASKED = -1e30
SCALE = HEAD_DIM ** (-0.5)
F32 = jnp.float32
BF16 = jnp.bfloat16
NT = (((1,), (1,)), ((), ()))


def normalize(matrix):
    values = matrix.astype(F32)
    inverse = lax.rsqrt(jnp.mean(values * values, axis=-1, keepdims=True) + EPSILON)
    return (values * inverse).astype(BF16)


def dot(a, b):
    return jnp.dot(a, b, preferred_element_type=F32)


def iota(shape, dim):
    return lax.broadcasted_iota(jnp.int32, shape, dim)


def onehot(condition):
    return jnp.where(condition, 1.0, 0.0).astype(BF16)


def stack_heads(q_pair):
    low = iota(q_pair.shape, 1) < HEAD_DIM
    zero = jnp.zeros_like(q_pair)
    return jnp.concatenate([jnp.where(low, q_pair, zero), jnp.where(low, zero, q_pair)], axis=0)


def unstack_heads(stacked):
    rows = stacked.shape[0] // 2
    low = iota((rows, PAIR), 1) < HEAD_DIM
    return jnp.where(low, stacked[:rows], stacked[rows:])


def kernel(
    n, tokens_hbm, boundary_hbm, wqf_hbm, wof_hbm, wqs_hbm, wos_hbm, out,
    tokens, boundary, wqf, wof, wqs, wos, prev, kv_cat, edges, marks, parted, joined,
    kv_all, mix, mix_tail,
    w_sem, tok_s, tok_r, edge_s, edge_r, marks_s, marks_r, part_s, part_r,
    kv_s, kv_r, mix_s, mix_r, mt_s, mt_r,
):
    length, width = tokens.shape
    capacity = length // 2
    groups = n // GROUP
    me = lax.axis_index("ctx")
    group = me // GROUP
    lane = lax.rem(me, GROUP)

    def remote(src, dst, s_sem, r_sem, device):
        return pltpu.make_async_remote_copy(
            src_ref=src, dst_ref=dst, send_sem=s_sem, recv_sem=r_sem,
            device_id={"ctx": device}, device_id_type=pl.DeviceIdType.MESH,
        )

    weights = [
        pltpu.make_async_copy(src, dst, w_sem.at[i])
        for i, (src, dst) in enumerate([
            (wqf_hbm, wqf), (wof_hbm, wof), (wqs_hbm, wqs), (wos_hbm, wos),
            (tokens_hbm, tokens), (boundary_hbm, boundary),
        ])
    ]

    barrier = pltpu.get_barrier_semaphore()

    def greet(k, carry):
        pl.semaphore_signal(
            barrier, inc=1, device_id={"ctx": lax.rem(me + k, n)}, device_id_type=pl.DeviceIdType.MESH
        )
        return carry

    lax.fori_loop(1, n, greet, 0)
    for i in (4, 5, 0, 1, 2, 3):
        weights[i].start()

    after = lax.rem(me + 1, n)
    before = lax.rem(me + n - 1, n)
    peers = [lax.rem(lane + k, GROUP) for k in range(1, GROUP)]
    weights[5].wait()
    bound = boundary[...]
    marks[lane] = jnp.broadcast_to(bound, (8, length))

    @pl.when(me == 0)
    def _():
        prev[...] = jnp.zeros_like(prev)

    @pl.when(group == groups - 1)
    def _():
        edges[GROUP] = jnp.zeros(edges.shape[1:], F32)

    @pl.when((lane != 0) | (group == 0))
    def _():
        edges[GROUP + 1] = jnp.zeros(edges.shape[1:], F32)

    @pl.when((lane != 0) | (group == 0))
    def _():
        mix_tail[...] = jnp.zeros_like(mix_tail)

    bound_rows = jnp.broadcast_to(bound.astype(F32), (length, length)).astype(BF16)
    i0 = iota((length, length), 0)
    i1 = iota((length, length), 1)
    seg_lane = dot(bound_rows, onehot(i0 <= i1)).astype(jnp.int32) - 1
    seg_sub = lax.dot_general(onehot(i1 <= i0), bound_rows, NT, preferred_element_type=F32).astype(jnp.int32) - 1
    starts = jnp.sum(bound, axis=1, keepdims=True)

    weights[4].wait()
    tok = tokens[...]
    normed = normalize(tok)
    pl.semaphore_wait(barrier, n - 1)

    tok_copy = remote(tokens_hbm, prev, tok_s, tok_r, after)

    @pl.when(me < n - 1)
    def _():
        tok_copy.start()

    marks_copies = [
        remote(marks.at[lane], marks.at[lane], marks_s.at[k], marks_r.at[lane], group * GROUP + peer)
        for k, peer in enumerate(peers)
    ]
    for copy in marks_copies:
        copy.start()

    weights[0].wait()
    packed = dot(normed, wqf[...]).astype(BF16)
    queries = packed[:, :INNER]
    kv_cat[length:, :] = packed[:, INNER:]

    @pl.when(me > 0)
    def _():
        remote(tokens_hbm, prev, tok_s, tok_r, before).wait_recv()

    kv_cat[:length, :] = dot(normalize(prev[...]), wqf[:, INNER:]).astype(BF16)

    q_pos = iota((length, 2 * length), 0) + length
    k_pos = iota((length, 2 * length), 1)
    first_key = jnp.where(me == 0, length, 0)
    allowed = (k_pos <= q_pos) & (k_pos > q_pos - WINDOW) & (k_pos >= first_key)
    allowed = jnp.concatenate([allowed, allowed], axis=0)
    mixed = []
    for p in range(HEADS // 2):
        cols = slice(p * PAIR, (p + 1) * PAIR)
        scores = lax.dot_general(stack_heads(queries[:, cols]), kv_cat[:, cols], NT, preferred_element_type=F32)
        scores = jnp.where(allowed, scores, MASKED)
        highest = jnp.max(scores, axis=-1, keepdims=True)
        expsum = jnp.exp((scores - highest) * SCALE)
        total = jnp.sum(expsum, axis=-1, keepdims=True)
        values = kv_cat[:, INNER + p * PAIR:INNER + (p + 1) * PAIR]
        mixed.append(unstack_heads(dot(expsum.astype(BF16), values) / total).astype(BF16))
    weights[1].wait()
    stream = (tok.astype(F32) + dot(jnp.concatenate(mixed, axis=1), wof[...])).astype(BF16)

    slot = iota((capacity, length), 0)
    gather = onehot(slot == seg_lane[:capacity])
    edge_row = iota((TAIL, length), 0)
    edge_seg = jnp.where(edge_row == 0, starts - 1, jnp.where(edge_row == 1, -1, starts - 2))
    edge_gather = onehot((edge_row < 3) & (edge_seg == seg_lane[:TAIL]))
    edge_sum = dot(edge_gather, stream)
    edge_size = jnp.sum(edge_gather.astype(F32), axis=1, keepdims=True)
    for r in range(3):
        edges[lane, r, :, :width] = edge_sum[r:r + 1]
        edges[lane, r, :, width:] = jnp.broadcast_to(edge_size[r:r + 1], (1, 128))
    edge_copies = [
        remote(edges.at[lane], edges.at[lane], edge_s.at[k], edge_r.at[lane], group * GROUP + peer)
        for k, peer in enumerate(peers)
    ]
    down_copies = [
        remote(edges.at[lane], edges.at[GROUP], edge_s.at[GROUP + j], edge_r.at[GROUP], lax.rem(me + n - GROUP + j, n))
        for j in range(GROUP)
    ]
    up_copy = remote(edges.at[lane], edges.at[GROUP + 1], edge_s.at[GROUP - 1], edge_r.at[GROUP + 1], after)
    sends_down = (lane == 0) & (group > 0)
    sends_up = (lane == GROUP - 1) & (group < groups - 1)
    for copy in edge_copies:
        copy.start()

    @pl.when(sends_down)
    def _():
        for copy in down_copies:
            copy.start()

    @pl.when(sends_up)
    def _():
        up_copy.start()

    partial = dot(gather, stream)
    sizes = jnp.sum(gather.astype(F32), axis=1, keepdims=True)
    pooled = (partial / jnp.maximum(sizes, 1.0)).astype(BF16)
    weights[2].wait()

    short = dot(normalize(pooled), wqs[...]).astype(BF16)
    for j in range(GROUP):
        for part in range(3):
            parted[j, :, part * PAIR:(part + 1) * PAIR] = short[:, part * INNER + j * PAIR:part * INNER + (j + 1) * PAIR]
    part_copies = [
        remote(parted.at[peer], joined.at[lane], part_s.at[k], part_r.at[lane], group * GROUP + peer)
        for k, peer in enumerate(peers)
    ]
    for copy in part_copies:
        copy.start()
    joined[lane] = parted[lane]

    for k, peer in enumerate(peers):
        remote(marks.at[lane], marks.at[peer], marks_s.at[k], marks_r.at[peer], group * GROUP + peer).wait_recv()
    counts = [jnp.sum(marks[j][0:1], axis=1, keepdims=True) for j in range(GROUP)]
    firsts = [jnp.zeros_like(counts[0])]
    for j in range(GROUP - 1):
        firsts.append(firsts[-1] + counts[j])
    my_first = firsts[0]
    for j in range(1, GROUP):
        my_first = jnp.where(lane == j, firsts[j], my_first)

    place = iota((length, GROUP * capacity), 0)
    source = iota((length, GROUP * capacity), 1)
    owner_first = jnp.broadcast_to(firsts[0], place.shape)
    owner_count = jnp.broadcast_to(counts[0], place.shape)
    for j in range(1, GROUP):
        beyond = source >= j * capacity
        owner_first = jnp.where(beyond, firsts[j], owner_first)
        owner_count = jnp.where(beyond, counts[j], owner_count)
    within = source & (capacity - 1)
    compact = onehot((within < owner_count - 1) & (within + owner_first == place))

    for k, peer in enumerate(peers):
        remote(edges.at[lane], edges.at[peer], edge_s.at[k], edge_r.at[peer], group * GROUP + peer).wait_recv()

    @pl.when(group < groups - 1)
    def _():
        remote(edges.at[lane], edges.at[GROUP], edge_s.at[0], edge_r.at[GROUP], after).wait_recv()

    blank = jnp.zeros((TAIL - GROUP, width + 128), F32)
    closed = jnp.concatenate([edges[j, 0] for j in range(GROUP)] + [blank], axis=0)
    closed = closed + jnp.concatenate([edges[j + 1, 1] for j in range(GROUP)] + [blank], axis=0)
    closed = (closed[:, :width] / jnp.maximum(closed[:, width:width + 1], 1.0)).astype(BF16)
    closed = normalize(closed)
    closed_rows = jnp.concatenate(
        [
            dot(closed, wqs[:, pl.ds(pl.multiple_of(part * INNER + lane * PAIR, PAIR), PAIR)])
            for part in range(3)
        ],
        axis=1,
    ).astype(BF16)
    closed_id = iota((length, TAIL), 1)
    closed_place = jnp.full((length, TAIL), -1, jnp.int32)
    for j in range(GROUP):
        closed_place = jnp.where(closed_id == j, firsts[j] + counts[j] - 1, closed_place)
    closed_at = onehot(closed_place == iota((length, TAIL), 0))

    for k, peer in enumerate(peers):
        remote(parted.at[lane], joined.at[peer], part_s.at[k], part_r.at[peer], group * GROUP + peer).wait_recv()
    rows = (dot(compact, joined[...].reshape(GROUP * capacity, 3 * PAIR)) + dot(closed_at, closed_rows)).astype(BF16)
    kv_all[group] = rows[:, PAIR:]

    def kv_copy(other):
        return remote(kv_all.at[group], kv_all.at[group], kv_s.at[other], kv_r.at[group], other * GROUP + lane)

    def send(other, carry):
        kv_copy(other).start()
        return carry

    lax.fori_loop(group + 1, groups, send, 0)

    q_stack = stack_heads(rows[:, :PAIR])
    scores = lax.dot_general(q_stack, rows[:, PAIR:2 * PAIR], NT, preferred_element_type=F32)
    causal = i1 <= i0
    scores = jnp.where(jnp.concatenate([causal, causal], axis=0), scores, MASKED)
    row_max = jnp.max(scores, axis=-1, keepdims=True)
    expsum = jnp.exp((scores - row_max) * SCALE)
    row_total = jnp.sum(expsum, axis=-1, keepdims=True)
    running = dot(expsum.astype(BF16), rows[:, 2 * PAIR:])

    @pl.when((lane == 0) & (group > 0))
    def _():
        remote(edges.at[lane], edges.at[GROUP + 1], edge_s.at[0], edge_r.at[GROUP + 1], before).wait_recv()

    behind = jnp.where(lane == 0, GROUP + 1, lane - 1)
    last = edges[behind, 0] + edges[lane, 1]
    last_two = jnp.concatenate([last, edges[behind, 2], jnp.zeros((TAIL - 2, width + 128), F32)], axis=0)
    last_two = (last_two[:, :width] / jnp.maximum(last_two[:, width:width + 1], 1.0)).astype(BF16)
    lift = onehot(iota((length, capacity), 1) == seg_sub[:, :capacity] - 1)
    lift_tail = onehot(iota((length, TAIL), 1) == -seg_sub[:, :TAIL])
    pooled_lifted = dot(lift, pooled) + dot(lift_tail, last_two)

    def attend(step, carry):
        row_max, row_total, running = carry
        other = group - 1 - step
        remote(
            kv_all.at[other], kv_all.at[other], kv_s.at[other], kv_r.at[other], other * GROUP + lane
        ).wait_recv()
        block = kv_all[other]
        scores = lax.dot_general(q_stack, block[:, :PAIR], NT, preferred_element_type=F32)
        new_max = jnp.maximum(row_max, jnp.max(scores, axis=-1, keepdims=True))
        expsum = jnp.exp((scores - new_max) * SCALE)
        fading = jnp.exp((row_max - new_max) * SCALE)
        row_total = row_total * fading + jnp.sum(expsum, axis=-1, keepdims=True)
        running = running * fading + dot(expsum.astype(BF16), block[:, PAIR:])
        return new_max, row_total, running

    row_max, row_total, running = lax.fori_loop(0, group, attend, (row_max, row_total, running))
    mix[lane] = unstack_heads(running / row_total).astype(BF16)

    mix_copies = [
        remote(mix.at[lane], mix.at[lane], mix_s.at[k], mix_r.at[lane], group * GROUP + peer)
        for k, peer in enumerate(peers)
    ]
    for copy in mix_copies:
        copy.start()
    next_lead = lax.rem((group + 1) * GROUP, n)
    mt_copy = remote(
        mix.at[lane, pl.ds(length - TAIL, TAIL)], mix_tail.at[lane], mt_s, mt_r.at[lane], next_lead
    )

    @pl.when(group < groups - 1)
    def _():
        mt_copy.start()

    weights[3].wait()
    target = seg_sub + my_first - 1
    pick = onehot(i1 == target)
    pick_tail = onehot(iota((length, TAIL), 1) == target[:, :TAIL] + TAIL)
    for k, peer in enumerate(peers):
        remote(mix.at[peer], mix.at[peer], mix_s.at[k], mix_r.at[peer], group * GROUP + peer).wait_recv()

    @pl.when((lane == 0) & (group > 0))
    def _():
        for j in range(GROUP):
            remote(
                mix.at[j, pl.ds(length - TAIL, TAIL)], mix_tail.at[j], mt_s, mt_r.at[j], before
            ).wait_recv()

    mixed_rows = jnp.concatenate([mix[j] for j in range(GROUP)], axis=1)
    tail_rows = jnp.concatenate([mix_tail[j] for j in range(GROUP)], axis=1)
    lifted = (dot(pick, mixed_rows) + dot(pick_tail, tail_rows)).astype(BF16)
    short_out = (pooled_lifted + dot(lifted, wos[...])).astype(BF16)
    out[...] = (stream.astype(F32) + short_out.astype(F32)).astype(BF16)

    @pl.when(me < n - 1)
    def _():
        tok_copy.wait_send()

    @pl.when(sends_down)
    def _():
        for copy in down_copies:
            copy.wait_send()

    @pl.when(sends_up)
    def _():
        up_copy.wait_send()

    for copy in marks_copies + edge_copies + part_copies + mix_copies:
        copy.wait_send()

    def drain(other, carry):
        kv_copy(other).wait_send()
        return carry

    lax.fori_loop(group + 1, groups, drain, 0)

    @pl.when(group < groups - 1)
    def _():
        mt_copy.wait_send()


def shards(n, tokens, boundary, w_qkv_full, w_out_full, w_qkv_short, w_out_short):
    length, width = tokens.shape
    capacity = length // 2
    groups = n // GROUP
    vmem = pl.BlockSpec(memory_space=pltpu.VMEM)
    hbm = pl.BlockSpec(memory_space=pl.ANY)
    dma = pltpu.SemaphoreType.DMA
    return pl.pallas_call(
        functools.partial(kernel, n),
        out_shape=jax.ShapeDtypeStruct((length, width), BF16),
        in_specs=[hbm, hbm, hbm, hbm, hbm, hbm],
        out_specs=vmem,
        scratch_shapes=[
            pltpu.VMEM((length, width), BF16),
            pltpu.VMEM((1, length), jnp.int32),
            pltpu.VMEM(w_qkv_full.shape, BF16),
            pltpu.VMEM(w_out_full.shape, BF16),
            pltpu.VMEM(w_qkv_short.shape, BF16),
            pltpu.VMEM(w_out_short.shape, BF16),
            pltpu.VMEM((length, width), BF16),
            pltpu.VMEM((2 * length, 2 * INNER), BF16),
            pltpu.VMEM((GROUP + 2, 3, 1, width + 128), F32),
            pltpu.VMEM((GROUP, 8, length), jnp.int32),
            pltpu.VMEM((GROUP, capacity, 3 * PAIR), BF16),
            pltpu.VMEM((GROUP, capacity, 3 * PAIR), BF16),
            pltpu.VMEM((groups, length, 2 * PAIR), BF16),
            pltpu.VMEM((GROUP, length, PAIR), BF16),
            pltpu.VMEM((GROUP, TAIL, PAIR), BF16),
            dma((6,)),
            dma, dma,
            dma((2 * GROUP,)), dma((GROUP + 2,)),
            dma((GROUP,)), dma((GROUP,)),
            dma((GROUP,)), dma((GROUP,)),
            dma((groups,)), dma((groups,)),
            dma((GROUP,)), dma((GROUP,)),
            dma, dma((GROUP,)),
        ],
        compiler_params=pltpu.CompilerParams(
            collective_id=0, has_side_effects=True, vmem_limit_bytes=60 * 1024 * 1024
        ),
    )(tokens, boundary.reshape(1, length), w_qkv_full, w_out_full, w_qkv_short, w_out_short)


def solution(mesh):
    return jax.shard_map(
        functools.partial(shards, mesh.shape["ctx"]),
        mesh=mesh,
        in_specs=(P(("parts", "ctx"), None), P(("parts", "ctx")), P(), P(), P(), P()),
        out_specs=P(("parts", "ctx"), None),
        check_vma=False,
    )
```

```python
import functools

import jax
import jax.numpy as jnp
from jax import lax
from jax.experimental import pallas as pl
from jax.experimental.pallas import tpu as pltpu
from jax.sharding import PartitionSpec as P

HEADS = 8
HEAD_DIM = 64
WINDOW = 128
INNER = HEADS * HEAD_DIM
PAIR = 2 * HEAD_DIM
GROUP = 4
TAIL = 16
EPSILON = 1e-06
MASKED = -1e30
SCALE = HEAD_DIM ** (-0.5)
F32 = jnp.float32
BF16 = jnp.bfloat16
NT = (((1,), (1,)), ((), ()))


def normalize(matrix):
    values = matrix.astype(F32)
    inverse = lax.rsqrt(jnp.mean(values * values, axis=-1, keepdims=True) + EPSILON)
    return (values * inverse).astype(BF16)


def dot(a, b):
    return jnp.dot(a, b, preferred_element_type=F32)


def iota(shape, dim):
    return lax.broadcasted_iota(jnp.int32, shape, dim)


def onehot(condition):
    return jnp.where(condition, 1.0, 0.0).astype(BF16)


def stack_heads(q_pair):
    low = iota(q_pair.shape, 1) < HEAD_DIM
    zero = jnp.zeros_like(q_pair)
    return jnp.concatenate([jnp.where(low, q_pair, zero), jnp.where(low, zero, q_pair)], axis=0)


def unstack_heads(stacked):
    rows = stacked.shape[0] // 2
    low = iota((rows, PAIR), 1) < HEAD_DIM
    return jnp.where(low, stacked[:rows], stacked[rows:])


def kernel(
    n, tokens_hbm, boundary_hbm, wqf_hbm, wof_hbm, wqs_hbm, wos_hbm, out,
    tokens, boundary, wqf, wof, wqs, wos, prev, kv_cat, edges, marks, parted, joined,
    kv_all, mix, mix_tail,
    above, w_sem, tok_s, tok_r, edge_s, edge_r, marks_s, marks_r, part_s, part_r,
    kv_s, kv_r, mix_s, mix_r, mt_s, mt_r,
):
    length, width = tokens.shape
    capacity = length // 2
    groups = n // GROUP
    me = lax.axis_index("ctx")
    group = me // GROUP
    lane = lax.rem(me, GROUP)

    def remote(src, dst, s_sem, r_sem, device):
        return pltpu.make_async_remote_copy(
            src_ref=src, dst_ref=dst, send_sem=s_sem, recv_sem=r_sem,
            device_id={"ctx": device}, device_id_type=pl.DeviceIdType.MESH,
        )

    weights = [
        pltpu.make_async_copy(src, dst, w_sem.at[i])
        for i, (src, dst) in enumerate([
            (wqf_hbm, wqf), (wof_hbm, wof), (wqs_hbm, wqs), (wos_hbm, wos),
            (tokens_hbm, tokens), (boundary_hbm, boundary),
        ])
    ]

    barrier = pltpu.get_barrier_semaphore()

    def signal(semaphore, device):
        pl.semaphore_signal(semaphore, inc=1, device_id={"ctx": device}, device_id_type=pl.DeviceIdType.MESH)

    has_below = group > 0
    has_above = group < groups - 1
    for k in range(1, GROUP):
        signal(barrier, group * GROUP + lax.rem(lane + k, GROUP))

    @pl.when(has_above)
    def _():
        signal(barrier, me + GROUP)

    @pl.when(has_below)
    def _():
        signal(barrier, me - GROUP)

    @pl.when(has_above & (lane > 0))
    def _():
        signal(barrier, (group + 1) * GROUP)

    @pl.when(has_below & (lane == 0))
    def _():
        for k in range(1, GROUP):
            signal(barrier, me - k)

    greeted = (
        GROUP - 1
        + jnp.where(has_above, 1, 0)
        + jnp.where(has_below, 1, 0)
        + jnp.where(has_above & (lane > 0), 1, 0)
        + jnp.where(has_below & (lane == 0), GROUP - 1, 0)
    )
    for i in (4, 5, 0, 1, 2, 3):
        weights[i].start()

    after = lax.rem(me + 1, n)
    before = lax.rem(me + n - 1, n)
    peers = [lax.rem(lane + k, GROUP) for k in range(1, GROUP)]
    weights[5].wait()
    bound = boundary[...]
    marks[lane] = jnp.broadcast_to(bound, (8, length))

    @pl.when(me == 0)
    def _():
        prev[...] = jnp.zeros_like(prev)

    @pl.when(group == groups - 1)
    def _():
        edges[GROUP] = jnp.zeros(edges.shape[1:], F32)

    @pl.when((lane != 0) | (group == 0))
    def _():
        edges[GROUP + 1] = jnp.zeros(edges.shape[1:], F32)

    @pl.when((lane != 0) | (group == 0))
    def _():
        mix_tail[...] = jnp.zeros_like(mix_tail)

    bound_rows = jnp.broadcast_to(bound.astype(F32), (length, length)).astype(BF16)
    i0 = iota((length, length), 0)
    i1 = iota((length, length), 1)
    seg_lane = dot(bound_rows, onehot(i0 <= i1)).astype(jnp.int32) - 1
    seg_sub = lax.dot_general(onehot(i1 <= i0), bound_rows, NT, preferred_element_type=F32).astype(jnp.int32) - 1
    starts = jnp.sum(bound, axis=1, keepdims=True)

    weights[4].wait()
    tok = tokens[...]
    normed = normalize(tok)
    pl.semaphore_wait(barrier, greeted)

    tok_copy = remote(tokens_hbm, prev, tok_s, tok_r, after)

    @pl.when(me < n - 1)
    def _():
        tok_copy.start()

    marks_copies = [
        remote(marks.at[lane], marks.at[lane], marks_s.at[k], marks_r.at[lane], group * GROUP + peer)
        for k, peer in enumerate(peers)
    ]
    for copy in marks_copies:
        copy.start()

    weights[0].wait()
    packed = dot(normed, wqf[...]).astype(BF16)
    queries = packed[:, :INNER]
    kv_cat[length:, :] = packed[:, INNER:]

    @pl.when(has_below & has_above)
    def _():
        pl.semaphore_wait(above, 1)

    @pl.when(has_below)
    def _():
        signal(above, me - GROUP)

    @pl.when(me > 0)
    def _():
        remote(tokens_hbm, prev, tok_s, tok_r, before).wait_recv()

    kv_cat[:length, :] = dot(normalize(prev[...]), wqf[:, INNER:]).astype(BF16)

    q_pos = iota((length, 2 * length), 0) + length
    k_pos = iota((length, 2 * length), 1)
    first_key = jnp.where(me == 0, length, 0)
    allowed = (k_pos <= q_pos) & (k_pos > q_pos - WINDOW) & (k_pos >= first_key)
    allowed = jnp.concatenate([allowed, allowed], axis=0)
    mixed = []
    for p in range(HEADS // 2):
        cols = slice(p * PAIR, (p + 1) * PAIR)
        scores = lax.dot_general(stack_heads(queries[:, cols]), kv_cat[:, cols], NT, preferred_element_type=F32)
        scores = jnp.where(allowed, scores, MASKED)
        highest = jnp.max(scores, axis=-1, keepdims=True)
        expsum = jnp.exp((scores - highest) * SCALE)
        total = jnp.sum(expsum, axis=-1, keepdims=True)
        values = kv_cat[:, INNER + p * PAIR:INNER + (p + 1) * PAIR]
        mixed.append(unstack_heads(dot(expsum.astype(BF16), values) / total).astype(BF16))
    weights[1].wait()
    stream = (tok.astype(F32) + dot(jnp.concatenate(mixed, axis=1), wof[...])).astype(BF16)

    slot = iota((capacity, length), 0)
    gather = onehot(slot == seg_lane[:capacity])
    edge_row = iota((TAIL, length), 0)
    edge_seg = jnp.where(edge_row == 0, starts - 1, jnp.where(edge_row == 1, -1, starts - 2))
    edge_gather = onehot((edge_row < 3) & (edge_seg == seg_lane[:TAIL]))
    edge_sum = dot(edge_gather, stream)
    edge_size = jnp.sum(edge_gather.astype(F32), axis=1, keepdims=True)
    for r in range(3):
        edges[lane, r, :, :width] = edge_sum[r:r + 1]
        edges[lane, r, :, width:] = jnp.broadcast_to(edge_size[r:r + 1], (1, 128))
    edge_copies = [
        remote(edges.at[lane], edges.at[lane], edge_s.at[k], edge_r.at[lane], group * GROUP + peer)
        for k, peer in enumerate(peers)
    ]
    down_copies = [
        remote(edges.at[lane], edges.at[GROUP], edge_s.at[GROUP + j], edge_r.at[GROUP], lax.rem(me + n - GROUP + j, n))
        for j in range(GROUP)
    ]
    up_copy = remote(edges.at[lane], edges.at[GROUP + 1], edge_s.at[GROUP - 1], edge_r.at[GROUP + 1], after)
    sends_down = (lane == 0) & (group > 0)
    sends_up = (lane == GROUP - 1) & (group < groups - 1)
    for copy in edge_copies:
        copy.start()

    @pl.when(sends_down)
    def _():
        for copy in down_copies:
            copy.start()

    @pl.when(sends_up)
    def _():
        up_copy.start()

    partial = dot(gather, stream)
    sizes = jnp.sum(gather.astype(F32), axis=1, keepdims=True)
    pooled = (partial / jnp.maximum(sizes, 1.0)).astype(BF16)
    weights[2].wait()

    short = dot(normalize(pooled), wqs[...]).astype(BF16)
    for j in range(GROUP):
        for part in range(3):
            parted[j, :, part * PAIR:(part + 1) * PAIR] = short[:, part * INNER + j * PAIR:part * INNER + (j + 1) * PAIR]
    part_copies = [
        remote(parted.at[peer], joined.at[lane], part_s.at[k], part_r.at[lane], group * GROUP + peer)
        for k, peer in enumerate(peers)
    ]
    for copy in part_copies:
        copy.start()
    joined[lane] = parted[lane]

    for k, peer in enumerate(peers):
        remote(marks.at[lane], marks.at[peer], marks_s.at[k], marks_r.at[peer], group * GROUP + peer).wait_recv()
    counts = [jnp.sum(marks[j][0:1], axis=1, keepdims=True) for j in range(GROUP)]
    firsts = [jnp.zeros_like(counts[0])]
    for j in range(GROUP - 1):
        firsts.append(firsts[-1] + counts[j])
    my_first = firsts[0]
    for j in range(1, GROUP):
        my_first = jnp.where(lane == j, firsts[j], my_first)

    place = iota((length, GROUP * capacity), 0)
    source = iota((length, GROUP * capacity), 1)
    owner_first = jnp.broadcast_to(firsts[0], place.shape)
    owner_count = jnp.broadcast_to(counts[0], place.shape)
    for j in range(1, GROUP):
        beyond = source >= j * capacity
        owner_first = jnp.where(beyond, firsts[j], owner_first)
        owner_count = jnp.where(beyond, counts[j], owner_count)
    within = source & (capacity - 1)
    compact = onehot((within < owner_count - 1) & (within + owner_first == place))

    for k, peer in enumerate(peers):
        remote(edges.at[lane], edges.at[peer], edge_s.at[k], edge_r.at[peer], group * GROUP + peer).wait_recv()

    @pl.when(group < groups - 1)
    def _():
        remote(edges.at[lane], edges.at[GROUP], edge_s.at[0], edge_r.at[GROUP], after).wait_recv()

    blank = jnp.zeros((TAIL - GROUP, width + 128), F32)
    closed = jnp.concatenate([edges[j, 0] for j in range(GROUP)] + [blank], axis=0)
    closed = closed + jnp.concatenate([edges[j + 1, 1] for j in range(GROUP)] + [blank], axis=0)
    closed = (closed[:, :width] / jnp.maximum(closed[:, width:width + 1], 1.0)).astype(BF16)
    closed = normalize(closed)
    closed_rows = jnp.concatenate(
        [
            dot(closed, wqs[:, pl.ds(pl.multiple_of(part * INNER + lane * PAIR, PAIR), PAIR)])
            for part in range(3)
        ],
        axis=1,
    ).astype(BF16)
    closed_id = iota((length, TAIL), 1)
    closed_place = jnp.full((length, TAIL), -1, jnp.int32)
    for j in range(GROUP):
        closed_place = jnp.where(closed_id == j, firsts[j] + counts[j] - 1, closed_place)
    closed_at = onehot(closed_place == iota((length, TAIL), 0))

    for k, peer in enumerate(peers):
        remote(parted.at[lane], joined.at[peer], part_s.at[k], part_r.at[peer], group * GROUP + peer).wait_recv()
    rows = (dot(compact, joined[...].reshape(GROUP * capacity, 3 * PAIR)) + dot(closed_at, closed_rows)).astype(BF16)
    kv_all[group] = rows[:, PAIR:]

    @pl.when(has_above & (group == 0))
    def _():
        pl.semaphore_wait(above, 1)

    def kv_copy(other):
        return remote(kv_all.at[group], kv_all.at[group], kv_s.at[other], kv_r.at[group], other * GROUP + lane)

    def send(other, carry):
        kv_copy(other).start()
        return carry

    lax.fori_loop(group + 1, groups, send, 0)

    q_stack = stack_heads(rows[:, :PAIR])
    scores = lax.dot_general(q_stack, rows[:, PAIR:2 * PAIR], NT, preferred_element_type=F32)
    causal = i1 <= i0
    scores = jnp.where(jnp.concatenate([causal, causal], axis=0), scores, MASKED)
    row_max = jnp.max(scores, axis=-1, keepdims=True)
    expsum = jnp.exp((scores - row_max) * SCALE)
    row_total = jnp.sum(expsum, axis=-1, keepdims=True)
    running = dot(expsum.astype(BF16), rows[:, 2 * PAIR:])

    @pl.when((lane == 0) & (group > 0))
    def _():
        remote(edges.at[lane], edges.at[GROUP + 1], edge_s.at[0], edge_r.at[GROUP + 1], before).wait_recv()

    behind = jnp.where(lane == 0, GROUP + 1, lane - 1)
    last = edges[behind, 0] + edges[lane, 1]
    last_two = jnp.concatenate([last, edges[behind, 2], jnp.zeros((TAIL - 2, width + 128), F32)], axis=0)
    last_two = (last_two[:, :width] / jnp.maximum(last_two[:, width:width + 1], 1.0)).astype(BF16)
    lift = onehot(iota((length, capacity), 1) == seg_sub[:, :capacity] - 1)
    lift_tail = onehot(iota((length, TAIL), 1) == -seg_sub[:, :TAIL])
    pooled_lifted = dot(lift, pooled) + dot(lift_tail, last_two)

    def attend(step, carry):
        row_max, row_total, running = carry
        other = group - 1 - step
        remote(
            kv_all.at[other], kv_all.at[other], kv_s.at[other], kv_r.at[other], other * GROUP + lane
        ).wait_recv()
        block = kv_all[other]
        scores = lax.dot_general(q_stack, block[:, :PAIR], NT, preferred_element_type=F32)
        new_max = jnp.maximum(row_max, jnp.max(scores, axis=-1, keepdims=True))
        expsum = jnp.exp((scores - new_max) * SCALE)
        fading = jnp.exp((row_max - new_max) * SCALE)
        row_total = row_total * fading + jnp.sum(expsum, axis=-1, keepdims=True)
        running = running * fading + dot(expsum.astype(BF16), block[:, PAIR:])
        return new_max, row_total, running

    row_max, row_total, running = lax.fori_loop(0, group, attend, (row_max, row_total, running))
    mix[lane] = unstack_heads(running / row_total).astype(BF16)

    mix_copies = [
        remote(mix.at[lane], mix.at[lane], mix_s.at[k], mix_r.at[lane], group * GROUP + peer)
        for k, peer in enumerate(peers)
    ]
    for copy in mix_copies:
        copy.start()
    next_lead = lax.rem((group + 1) * GROUP, n)
    mt_copy = remote(
        mix.at[lane, pl.ds(length - TAIL, TAIL)], mix_tail.at[lane], mt_s, mt_r.at[lane], next_lead
    )

    @pl.when(group < groups - 1)
    def _():
        mt_copy.start()

    weights[3].wait()
    target = seg_sub + my_first - 1
    pick = onehot(i1 == target)
    pick_tail = onehot(iota((length, TAIL), 1) == target[:, :TAIL] + TAIL)
    for k, peer in enumerate(peers):
        remote(mix.at[peer], mix.at[peer], mix_s.at[k], mix_r.at[peer], group * GROUP + peer).wait_recv()

    @pl.when((lane == 0) & (group > 0))
    def _():
        for j in range(GROUP):
            remote(
                mix.at[j, pl.ds(length - TAIL, TAIL)], mix_tail.at[j], mt_s, mt_r.at[j], before
            ).wait_recv()

    mixed_rows = jnp.concatenate([mix[j] for j in range(GROUP)], axis=1)
    tail_rows = jnp.concatenate([mix_tail[j] for j in range(GROUP)], axis=1)
    lifted = (dot(pick, mixed_rows) + dot(pick_tail, tail_rows)).astype(BF16)
    short_out = (pooled_lifted + dot(lifted, wos[...])).astype(BF16)
    out[...] = (stream.astype(F32) + short_out.astype(F32)).astype(BF16)

    @pl.when(me < n - 1)
    def _():
        tok_copy.wait_send()

    @pl.when(sends_down)
    def _():
        for copy in down_copies:
            copy.wait_send()

    @pl.when(sends_up)
    def _():
        up_copy.wait_send()

    for copy in marks_copies + edge_copies + part_copies + mix_copies:
        copy.wait_send()

    def drain(other, carry):
        kv_copy(other).wait_send()
        return carry

    lax.fori_loop(group + 1, groups, drain, 0)

    @pl.when(group < groups - 1)
    def _():
        mt_copy.wait_send()


def shards(n, tokens, boundary, w_qkv_full, w_out_full, w_qkv_short, w_out_short):
    length, width = tokens.shape
    capacity = length // 2
    groups = n // GROUP
    vmem = pl.BlockSpec(memory_space=pltpu.VMEM)
    hbm = pl.BlockSpec(memory_space=pl.ANY)
    dma = pltpu.SemaphoreType.DMA
    return pl.pallas_call(
        functools.partial(kernel, n),
        out_shape=jax.ShapeDtypeStruct((length, width), BF16),
        in_specs=[hbm, hbm, hbm, hbm, hbm, hbm],
        out_specs=vmem,
        scratch_shapes=[
            pltpu.VMEM((length, width), BF16),
            pltpu.VMEM((1, length), jnp.int32),
            pltpu.VMEM(w_qkv_full.shape, BF16),
            pltpu.VMEM(w_out_full.shape, BF16),
            pltpu.VMEM(w_qkv_short.shape, BF16),
            pltpu.VMEM(w_out_short.shape, BF16),
            pltpu.VMEM((length, width), BF16),
            pltpu.VMEM((2 * length, 2 * INNER), BF16),
            pltpu.VMEM((GROUP + 2, 3, 1, width + 128), F32),
            pltpu.VMEM((GROUP, 8, length), jnp.int32),
            pltpu.VMEM((GROUP, capacity, 3 * PAIR), BF16),
            pltpu.VMEM((GROUP, capacity, 3 * PAIR), BF16),
            pltpu.VMEM((groups, length, 2 * PAIR), BF16),
            pltpu.VMEM((GROUP, length, PAIR), BF16),
            pltpu.VMEM((GROUP, TAIL, PAIR), BF16),
            pltpu.SemaphoreType.REGULAR,
            dma((6,)),
            dma, dma,
            dma((2 * GROUP,)), dma((GROUP + 2,)),
            dma((GROUP,)), dma((GROUP,)),
            dma((GROUP,)), dma((GROUP,)),
            dma((groups,)), dma((groups,)),
            dma((GROUP,)), dma((GROUP,)),
            dma, dma((GROUP,)),
        ],
        compiler_params=pltpu.CompilerParams(
            collective_id=0, has_side_effects=True, vmem_limit_bytes=60 * 1024 * 1024
        ),
    )(tokens, boundary.reshape(1, length), w_qkv_full, w_out_full, w_qkv_short, w_out_short)


def solution(mesh):
    return jax.shard_map(
        functools.partial(shards, mesh.shape["ctx"]),
        mesh=mesh,
        in_specs=(P(("parts", "ctx"), None), P(("parts", "ctx")), P(), P(), P(), P()),
        out_specs=P(("parts", "ctx"), None),
        check_vma=False,
    )
```

```python
import functools

import jax
import jax.numpy as jnp
from jax import lax
from jax.experimental import pallas as pl
from jax.experimental.pallas import tpu as pltpu
from jax.sharding import PartitionSpec as P

HEADS = 8
HEAD_DIM = 64
WINDOW = 128
INNER = HEADS * HEAD_DIM
PAIR = 2 * HEAD_DIM
GROUP = 4
TAIL = 16
EPSILON = 1e-06
MASKED = -1e30
SCALE = HEAD_DIM ** (-0.5)
F32 = jnp.float32
BF16 = jnp.bfloat16
NT = (((1,), (1,)), ((), ()))


def normalize(matrix):
    values = matrix.astype(F32)
    inverse = lax.rsqrt(jnp.mean(values * values, axis=-1, keepdims=True) + EPSILON)
    return (values * inverse).astype(BF16)


def dot(a, b):
    return jnp.dot(a, b, preferred_element_type=F32)


def iota(shape, dim):
    return lax.broadcasted_iota(jnp.int32, shape, dim)


def onehot(condition):
    return jnp.where(condition, 1.0, 0.0).astype(BF16)


def stack_heads(q_pair):
    low = iota(q_pair.shape, 1) < HEAD_DIM
    zero = jnp.zeros_like(q_pair)
    return jnp.concatenate([jnp.where(low, q_pair, zero), jnp.where(low, zero, q_pair)], axis=0)


def unstack_heads(stacked):
    rows = stacked.shape[0] // 2
    low = iota((rows, PAIR), 1) < HEAD_DIM
    return jnp.where(low, stacked[:rows], stacked[rows:])


def kernel(
    n, tokens_hbm, boundary_hbm, wqf_hbm, wof_hbm, wqs_hbm, wos_hbm, out,
    tokens, boundary, wqf, wof, wqs, wos, prev, kv_cat, edges, marks, parted, joined,
    kv_all, mix, mix_tail,
    above, w_sem, tok_s, tok_r, edge_s, edge_r, marks_s, marks_r, part_s, part_r,
    kv_s, kv_r, mix_s, mix_r, mt_s, mt_r,
):
    length, width = tokens.shape
    capacity = length // 2
    groups = n // GROUP
    me = lax.axis_index("ctx")
    group = me // GROUP
    lane = lax.rem(me, GROUP)

    def remote(src, dst, s_sem, r_sem, device):
        return pltpu.make_async_remote_copy(
            src_ref=src, dst_ref=dst, send_sem=s_sem, recv_sem=r_sem,
            device_id={"ctx": device}, device_id_type=pl.DeviceIdType.MESH,
        )

    weights = [
        pltpu.make_async_copy(src, dst, w_sem.at[i])
        for i, (src, dst) in enumerate([
            (wqf_hbm, wqf), (wof_hbm, wof), (wqs_hbm, wqs), (wos_hbm, wos),
            (tokens_hbm, tokens), (boundary_hbm, boundary),
        ])
    ]

    barrier = pltpu.get_barrier_semaphore()

    def signal(semaphore, device):
        pl.semaphore_signal(semaphore, inc=1, device_id={"ctx": device}, device_id_type=pl.DeviceIdType.MESH)

    has_below = group > 0
    has_above = group < groups - 1
    for k in range(1, GROUP):
        signal(barrier, group * GROUP + lax.rem(lane + k, GROUP))

    @pl.when(has_above)
    def _():
        signal(barrier, me + GROUP)

    @pl.when(has_below)
    def _():
        signal(barrier, me - GROUP)

    @pl.when(has_above & (lane > 0))
    def _():
        signal(barrier, (group + 1) * GROUP)

    @pl.when(has_below & (lane == 0))
    def _():
        for k in range(1, GROUP):
            signal(barrier, me - k)

    greeted = (
        GROUP - 1
        + jnp.where(has_above, 1, 0)
        + jnp.where(has_below, 1, 0)
        + jnp.where(has_above & (lane > 0), 1, 0)
        + jnp.where(has_below & (lane == 0), GROUP - 1, 0)
    )
    for i in (4, 5, 0):
        weights[i].start()

    after = lax.rem(me + 1, n)
    before = lax.rem(me + n - 1, n)
    peers = [lax.rem(lane + k, GROUP) for k in range(1, GROUP)]
    weights[5].wait()
    bound = boundary[...]
    marks[lane] = jnp.broadcast_to(bound, (8, length))

    @pl.when(me == 0)
    def _():
        prev[...] = jnp.zeros_like(prev)

    @pl.when(group == groups - 1)
    def _():
        edges[GROUP] = jnp.zeros(edges.shape[1:], F32)

    @pl.when((lane != 0) | (group == 0))
    def _():
        edges[GROUP + 1] = jnp.zeros(edges.shape[1:], F32)

    @pl.when((lane != 0) | (group == 0))
    def _():
        mix_tail[...] = jnp.zeros_like(mix_tail)

    bound_rows = jnp.broadcast_to(bound.astype(F32), (length, length)).astype(BF16)
    i0 = iota((length, length), 0)
    i1 = iota((length, length), 1)
    seg_lane = dot(bound_rows, onehot(i0 <= i1)).astype(jnp.int32) - 1
    seg_sub = lax.dot_general(onehot(i1 <= i0), bound_rows, NT, preferred_element_type=F32).astype(jnp.int32) - 1
    starts = jnp.sum(bound, axis=1, keepdims=True)

    weights[4].wait()
    tok = tokens[...]
    normed = normalize(tok)
    pl.semaphore_wait(barrier, greeted)

    tok_copy = remote(tokens, prev, tok_s, tok_r, after)

    @pl.when(me < n - 1)
    def _():
        tok_copy.start()

    marks_copies = [
        remote(marks.at[lane], marks.at[lane], marks_s.at[k], marks_r.at[lane], group * GROUP + peer)
        for k, peer in enumerate(peers)
    ]
    for copy in marks_copies:
        copy.start()
    for i in (1, 2, 3):
        weights[i].start()

    weights[0].wait()
    packed = dot(normed, wqf[...]).astype(BF16)
    queries = packed[:, :INNER]
    kv_cat[length:, :] = packed[:, INNER:]

    @pl.when(has_below & has_above)
    def _():
        pl.semaphore_wait(above, 1)

    @pl.when(has_below)
    def _():
        signal(above, me - GROUP)

    @pl.when(me > 0)
    def _():
        remote(tokens, prev, tok_s, tok_r, before).wait_recv()

    kv_cat[:length, :] = dot(normalize(prev[...]), wqf[:, INNER:]).astype(BF16)

    q_pos = iota((length, 2 * length), 0) + length
    k_pos = iota((length, 2 * length), 1)
    first_key = jnp.where(me == 0, length, 0)
    allowed = (k_pos <= q_pos) & (k_pos > q_pos - WINDOW) & (k_pos >= first_key)
    allowed = jnp.concatenate([allowed, allowed], axis=0)
    mixed = []
    for p in range(HEADS // 2):
        cols = slice(p * PAIR, (p + 1) * PAIR)
        scores = lax.dot_general(stack_heads(queries[:, cols]), kv_cat[:, cols], NT, preferred_element_type=F32)
        scores = jnp.where(allowed, scores, MASKED)
        highest = jnp.max(scores, axis=-1, keepdims=True)
        expsum = jnp.exp((scores - highest) * SCALE)
        total = jnp.sum(expsum, axis=-1, keepdims=True)
        values = kv_cat[:, INNER + p * PAIR:INNER + (p + 1) * PAIR]
        mixed.append(unstack_heads(dot(expsum.astype(BF16), values) / total).astype(BF16))
    weights[1].wait()
    stream = (tok.astype(F32) + dot(jnp.concatenate(mixed, axis=1), wof[...])).astype(BF16)

    slot = iota((capacity, length), 0)
    gather = onehot(slot == seg_lane[:capacity])
    edge_row = iota((TAIL, length), 0)
    edge_seg = jnp.where(edge_row == 0, starts - 1, jnp.where(edge_row == 1, -1, starts - 2))
    edge_gather = onehot((edge_row < 3) & (edge_seg == seg_lane[:TAIL]))
    edge_sum = dot(edge_gather, stream)
    edge_size = jnp.sum(edge_gather.astype(F32), axis=1, keepdims=True)
    for r in range(3):
        edges[lane, r, :, :width] = edge_sum[r:r + 1]
        edges[lane, r, :, width:] = jnp.broadcast_to(edge_size[r:r + 1], (1, 128))
    edge_copies = [
        remote(edges.at[lane], edges.at[lane], edge_s.at[k], edge_r.at[lane], group * GROUP + peer)
        for k, peer in enumerate(peers)
    ]
    down_copies = [
        remote(edges.at[lane], edges.at[GROUP], edge_s.at[GROUP + j], edge_r.at[GROUP], lax.rem(me + n - GROUP + j, n))
        for j in range(GROUP)
    ]
    up_copy = remote(edges.at[lane], edges.at[GROUP + 1], edge_s.at[GROUP - 1], edge_r.at[GROUP + 1], after)
    sends_down = (lane == 0) & (group > 0)
    sends_up = (lane == GROUP - 1) & (group < groups - 1)
    for copy in edge_copies:
        copy.start()

    @pl.when(sends_down)
    def _():
        for copy in down_copies:
            copy.start()

    @pl.when(sends_up)
    def _():
        up_copy.start()

    partial = dot(gather, stream)
    sizes = jnp.sum(gather.astype(F32), axis=1, keepdims=True)
    pooled = (partial / jnp.maximum(sizes, 1.0)).astype(BF16)
    weights[2].wait()

    short = dot(normalize(pooled), wqs[...]).astype(BF16)
    for j in range(GROUP):
        for part in range(3):
            parted[j, :, part * PAIR:(part + 1) * PAIR] = short[:, part * INNER + j * PAIR:part * INNER + (j + 1) * PAIR]
    part_copies = [
        remote(parted.at[peer], joined.at[lane], part_s.at[k], part_r.at[lane], group * GROUP + peer)
        for k, peer in enumerate(peers)
    ]
    for copy in part_copies:
        copy.start()
    joined[lane] = parted[lane]

    for k, peer in enumerate(peers):
        remote(marks.at[lane], marks.at[peer], marks_s.at[k], marks_r.at[peer], group * GROUP + peer).wait_recv()
    counts = [jnp.sum(marks[j][0:1], axis=1, keepdims=True) for j in range(GROUP)]
    firsts = [jnp.zeros_like(counts[0])]
    for j in range(GROUP - 1):
        firsts.append(firsts[-1] + counts[j])
    my_first = firsts[0]
    for j in range(1, GROUP):
        my_first = jnp.where(lane == j, firsts[j], my_first)

    place = iota((length, GROUP * capacity), 0)
    source = iota((length, GROUP * capacity), 1)
    owner_first = jnp.broadcast_to(firsts[0], place.shape)
    owner_count = jnp.broadcast_to(counts[0], place.shape)
    for j in range(1, GROUP):
        beyond = source >= j * capacity
        owner_first = jnp.where(beyond, firsts[j], owner_first)
        owner_count = jnp.where(beyond, counts[j], owner_count)
    within = source & (capacity - 1)
    compact = onehot((within < owner_count - 1) & (within + owner_first == place))

    for k, peer in enumerate(peers):
        remote(edges.at[lane], edges.at[peer], edge_s.at[k], edge_r.at[peer], group * GROUP + peer).wait_recv()

    @pl.when(group < groups - 1)
    def _():
        remote(edges.at[lane], edges.at[GROUP], edge_s.at[0], edge_r.at[GROUP], after).wait_recv()

    blank = jnp.zeros((TAIL - GROUP, width + 128), F32)
    closed = jnp.concatenate([edges[j, 0] for j in range(GROUP)] + [blank], axis=0)
    closed = closed + jnp.concatenate([edges[j + 1, 1] for j in range(GROUP)] + [blank], axis=0)
    closed = (closed[:, :width] / jnp.maximum(closed[:, width:width + 1], 1.0)).astype(BF16)
    closed = normalize(closed)
    closed_rows = jnp.concatenate(
        [
            dot(closed, wqs[:, pl.ds(pl.multiple_of(part * INNER + lane * PAIR, PAIR), PAIR)])
            for part in range(3)
        ],
        axis=1,
    ).astype(BF16)
    closed_id = iota((length, TAIL), 1)
    closed_place = jnp.full((length, TAIL), -1, jnp.int32)
    for j in range(GROUP):
        closed_place = jnp.where(closed_id == j, firsts[j] + counts[j] - 1, closed_place)
    closed_at = onehot(closed_place == iota((length, TAIL), 0))

    for k, peer in enumerate(peers):
        remote(parted.at[lane], joined.at[peer], part_s.at[k], part_r.at[peer], group * GROUP + peer).wait_recv()
    rows = (dot(compact, joined[...].reshape(GROUP * capacity, 3 * PAIR)) + dot(closed_at, closed_rows)).astype(BF16)
    kv_all[group] = rows[:, PAIR:]

    @pl.when(has_above & (group == 0))
    def _():
        pl.semaphore_wait(above, 1)

    def kv_copy(other):
        return remote(kv_all.at[group], kv_all.at[group], kv_s.at[other], kv_r.at[group], other * GROUP + lane)

    def send(step, carry):
        kv_copy(groups + group - step).start()
        return carry

    lax.fori_loop(group + 1, groups, send, 0)

    q_stack = stack_heads(rows[:, :PAIR])
    scores = lax.dot_general(q_stack, rows[:, PAIR:2 * PAIR], NT, preferred_element_type=F32)
    causal = i1 <= i0
    scores = jnp.where(jnp.concatenate([causal, causal], axis=0), scores, MASKED)
    row_max = jnp.max(scores, axis=-1, keepdims=True)
    expsum = jnp.exp((scores - row_max) * SCALE)
    row_total = jnp.sum(expsum, axis=-1, keepdims=True)
    running = dot(expsum.astype(BF16), rows[:, 2 * PAIR:])

    @pl.when((lane == 0) & (group > 0))
    def _():
        remote(edges.at[lane], edges.at[GROUP + 1], edge_s.at[0], edge_r.at[GROUP + 1], before).wait_recv()

    behind = jnp.where(lane == 0, GROUP + 1, lane - 1)
    last = edges[behind, 0] + edges[lane, 1]
    last_two = jnp.concatenate([last, edges[behind, 2], jnp.zeros((TAIL - 2, width + 128), F32)], axis=0)
    last_two = (last_two[:, :width] / jnp.maximum(last_two[:, width:width + 1], 1.0)).astype(BF16)
    lift = onehot(iota((length, capacity), 1) == seg_sub[:, :capacity] - 1)
    lift_tail = onehot(iota((length, TAIL), 1) == -seg_sub[:, :TAIL])
    pooled_lifted = dot(lift, pooled) + dot(lift_tail, last_two)

    def attend(step, carry):
        row_max, row_total, running = carry
        other = group - 1 - step
        remote(
            kv_all.at[other], kv_all.at[other], kv_s.at[other], kv_r.at[other], other * GROUP + lane
        ).wait_recv()
        block = kv_all[other]
        scores = lax.dot_general(q_stack, block[:, :PAIR], NT, preferred_element_type=F32)
        new_max = jnp.maximum(row_max, jnp.max(scores, axis=-1, keepdims=True))
        expsum = jnp.exp((scores - new_max) * SCALE)
        fading = jnp.exp((row_max - new_max) * SCALE)
        row_total = row_total * fading + jnp.sum(expsum, axis=-1, keepdims=True)
        running = running * fading + dot(expsum.astype(BF16), block[:, PAIR:])
        return new_max, row_total, running

    row_max, row_total, running = lax.fori_loop(0, group, attend, (row_max, row_total, running))
    mix[lane] = unstack_heads(running / row_total).astype(BF16)

    mix_copies = [
        remote(mix.at[lane], mix.at[lane], mix_s.at[k], mix_r.at[lane], group * GROUP + peer)
        for k, peer in enumerate(peers)
    ]
    for copy in mix_copies:
        copy.start()
    next_lead = lax.rem((group + 1) * GROUP, n)
    mt_copy = remote(
        mix.at[lane, pl.ds(length - TAIL, TAIL)], mix_tail.at[lane], mt_s, mt_r.at[lane], next_lead
    )

    @pl.when(group < groups - 1)
    def _():
        mt_copy.start()

    weights[3].wait()
    target = seg_sub + my_first - 1
    pick = onehot(i1 == target)
    pick_tail = onehot(iota((length, TAIL), 1) == target[:, :TAIL] + TAIL)
    for k, peer in enumerate(peers):
        remote(mix.at[peer], mix.at[peer], mix_s.at[k], mix_r.at[peer], group * GROUP + peer).wait_recv()

    @pl.when((lane == 0) & (group > 0))
    def _():
        for j in range(GROUP):
            remote(
                mix.at[j, pl.ds(length - TAIL, TAIL)], mix_tail.at[j], mt_s, mt_r.at[j], before
            ).wait_recv()

    mixed_rows = jnp.concatenate([mix[j] for j in range(GROUP)], axis=1)
    tail_rows = jnp.concatenate([mix_tail[j] for j in range(GROUP)], axis=1)
    lifted = (dot(pick, mixed_rows) + dot(pick_tail, tail_rows)).astype(BF16)
    short_out = (pooled_lifted + dot(lifted, wos[...])).astype(BF16)
    out[...] = (stream.astype(F32) + short_out.astype(F32)).astype(BF16)

    @pl.when(me < n - 1)
    def _():
        tok_copy.wait_send()

    @pl.when(sends_down)
    def _():
        for copy in down_copies:
            copy.wait_send()

    @pl.when(sends_up)
    def _():
        up_copy.wait_send()

    for copy in marks_copies + edge_copies + part_copies + mix_copies:
        copy.wait_send()

    def drain(other, carry):
        kv_copy(other).wait_send()
        return carry

    lax.fori_loop(group + 1, groups, drain, 0)

    @pl.when(group < groups - 1)
    def _():
        mt_copy.wait_send()


def shards(n, tokens, boundary, w_qkv_full, w_out_full, w_qkv_short, w_out_short):
    length, width = tokens.shape
    capacity = length // 2
    groups = n // GROUP
    vmem = pl.BlockSpec(memory_space=pltpu.VMEM)
    hbm = pl.BlockSpec(memory_space=pl.ANY)
    dma = pltpu.SemaphoreType.DMA
    return pl.pallas_call(
        functools.partial(kernel, n),
        out_shape=jax.ShapeDtypeStruct((length, width), BF16),
        in_specs=[hbm, hbm, hbm, hbm, hbm, hbm],
        out_specs=vmem,
        scratch_shapes=[
            pltpu.VMEM((length, width), BF16),
            pltpu.VMEM((1, length), jnp.int32),
            pltpu.VMEM(w_qkv_full.shape, BF16),
            pltpu.VMEM(w_out_full.shape, BF16),
            pltpu.VMEM(w_qkv_short.shape, BF16),
            pltpu.VMEM(w_out_short.shape, BF16),
            pltpu.VMEM((length, width), BF16),
            pltpu.VMEM((2 * length, 2 * INNER), BF16),
            pltpu.VMEM((GROUP + 2, 3, 1, width + 128), F32),
            pltpu.VMEM((GROUP, 8, length), jnp.int32),
            pltpu.VMEM((GROUP, capacity, 3 * PAIR), BF16),
            pltpu.VMEM((GROUP, capacity, 3 * PAIR), BF16),
            pltpu.VMEM((groups, length, 2 * PAIR), BF16),
            pltpu.VMEM((GROUP, length, PAIR), BF16),
            pltpu.VMEM((GROUP, TAIL, PAIR), BF16),
            pltpu.SemaphoreType.REGULAR,
            dma((6,)),
            dma, dma,
            dma((2 * GROUP,)), dma((GROUP + 2,)),
            dma((GROUP,)), dma((GROUP,)),
            dma((GROUP,)), dma((GROUP,)),
            dma((groups,)), dma((groups,)),
            dma((GROUP,)), dma((GROUP,)),
            dma, dma((GROUP,)),
        ],
        compiler_params=pltpu.CompilerParams(
            collective_id=0, has_side_effects=True, vmem_limit_bytes=54850 * 1024
        ),
    )(tokens, boundary.reshape(1, length), w_qkv_full, w_out_full, w_qkv_short, w_out_short)


def solution(mesh):
    return jax.shard_map(
        functools.partial(shards, mesh.shape["ctx"]),
        mesh=mesh,
        in_specs=(P(("parts", "ctx"), None), P(("parts", "ctx")), P(), P(), P(), P()),
        out_specs=P(("parts", "ctx"), None),
        check_vma=False,
    )
```

```python
import functools

import jax
import jax.numpy as jnp
from jax import lax
from jax.experimental import pallas as pl
from jax.experimental.pallas import tpu as pltpu
from jax.sharding import PartitionSpec as P

HEADS = 8
HEAD_DIM = 64
WINDOW = 128
INNER = HEADS * HEAD_DIM
PAIR = 2 * HEAD_DIM
GROUP = 4
TAIL = 16
EPSILON = 1e-06
MASKED = -1e30
SCALE = HEAD_DIM ** (-0.5)
F32 = jnp.float32
BF16 = jnp.bfloat16
NT = (((1,), (1,)), ((), ()))


def normalize(matrix):
    values = matrix.astype(F32)
    inverse = lax.rsqrt(jnp.mean(values * values, axis=-1, keepdims=True) + EPSILON)
    return (values * inverse).astype(BF16)


def dot(a, b):
    return jnp.dot(a, b, preferred_element_type=F32)


def iota(shape, dim):
    return lax.broadcasted_iota(jnp.int32, shape, dim)


def onehot(condition):
    return jnp.where(condition, 1.0, 0.0).astype(BF16)


def stack_heads(q_pair):
    low = iota(q_pair.shape, 1) < HEAD_DIM
    zero = jnp.zeros_like(q_pair)
    return jnp.concatenate([jnp.where(low, q_pair, zero), jnp.where(low, zero, q_pair)], axis=0)


def unstack_heads(stacked):
    rows = stacked.shape[0] // 2
    low = iota((rows, PAIR), 1) < HEAD_DIM
    return jnp.where(low, stacked[:rows], stacked[rows:])


def kernel(
    n, tokens_hbm, boundary_hbm, wqf_hbm, wof_hbm, wqs_hbm, wos_hbm, out,
    tokens, boundary, wqf, wof, wqs, wos, prev, kv_cat, edges, marks, parted, joined,
    kv_all, mix, mix_tail,
    above, w_sem, tok_s, tok_r, edge_s, edge_r, marks_s, marks_r, part_s, part_r,
    kv_s, kv_r, mix_s, mix_r, mt_s, mt_r,
):
    length, width = tokens.shape
    capacity = length // 2
    groups = n // GROUP
    me = lax.axis_index("ctx")
    group = me // GROUP
    lane = lax.rem(me, GROUP)

    def remote(src, dst, s_sem, r_sem, device):
        return pltpu.make_async_remote_copy(
            src_ref=src, dst_ref=dst, send_sem=s_sem, recv_sem=r_sem,
            device_id={"ctx": device}, device_id_type=pl.DeviceIdType.MESH,
        )

    weights = [
        pltpu.make_async_copy(src, dst, w_sem.at[i])
        for i, (src, dst) in enumerate([
            (wqf_hbm, wqf), (wof_hbm, wof), (wqs_hbm, wqs), (wos_hbm, wos),
            (tokens_hbm, tokens), (boundary_hbm, boundary),
        ])
    ]

    barrier = pltpu.get_barrier_semaphore()

    def signal(semaphore, device):
        pl.semaphore_signal(semaphore, inc=1, device_id={"ctx": device}, device_id_type=pl.DeviceIdType.MESH)

    has_below = group > 0
    has_above = group < groups - 1
    for k in range(1, GROUP):
        signal(barrier, group * GROUP + lax.rem(lane + k, GROUP))

    @pl.when(has_above)
    def _():
        signal(barrier, me + GROUP)

    @pl.when(has_below)
    def _():
        signal(barrier, me - GROUP)

    @pl.when(has_above & (lane > 0))
    def _():
        signal(barrier, (group + 1) * GROUP)

    @pl.when(has_below & (lane == 0))
    def _():
        for k in range(1, GROUP):
            signal(barrier, me - k)

    greeted = (
        GROUP - 1
        + jnp.where(has_above, 1, 0)
        + jnp.where(has_below, 1, 0)
        + jnp.where(has_above & (lane > 0), 1, 0)
        + jnp.where(has_below & (lane == 0), GROUP - 1, 0)
    )
    for i in (4, 5, 0):
        weights[i].start()

    after = lax.rem(me + 1, n)
    before = lax.rem(me + n - 1, n)
    odd = lax.rem(lane, 2)
    peers = [lax.rem(lane + 2, GROUP), lax.rem(lane + 3 - 2 * odd, GROUP), lax.rem(lane + 1 + 2 * odd, GROUP)]
    weights[5].wait()
    bound = boundary[...]
    marks[lane] = jnp.broadcast_to(bound, (8, length))

    @pl.when(me == 0)
    def _():
        prev[...] = jnp.zeros_like(prev)

    @pl.when(group == groups - 1)
    def _():
        edges[GROUP] = jnp.zeros(edges.shape[1:], F32)

    @pl.when((lane != 0) | (group == 0))
    def _():
        edges[GROUP + 1] = jnp.zeros(edges.shape[1:], F32)

    @pl.when((lane != 0) | (group == 0))
    def _():
        mix_tail[...] = jnp.zeros_like(mix_tail)

    bound_rows = jnp.broadcast_to(bound.astype(F32), (length, length)).astype(BF16)
    i0 = iota((length, length), 0)
    i1 = iota((length, length), 1)
    seg_lane = dot(bound_rows, onehot(i0 <= i1)).astype(jnp.int32) - 1
    seg_sub = lax.dot_general(onehot(i1 <= i0), bound_rows, NT, preferred_element_type=F32).astype(jnp.int32) - 1
    starts = jnp.sum(bound, axis=1, keepdims=True)

    weights[4].wait()
    tok = tokens[...]
    normed = normalize(tok)
    pl.semaphore_wait(barrier, greeted)

    tok_copy = remote(tokens, prev, tok_s, tok_r, after)

    @pl.when(me < n - 1)
    def _():
        tok_copy.start()

    marks_copies = [
        remote(marks.at[lane], marks.at[lane], marks_s.at[k], marks_r.at[lane], group * GROUP + peer)
        for k, peer in enumerate(peers)
    ]
    for copy in marks_copies:
        copy.start()
    for i in (1, 2, 3):
        weights[i].start()

    weights[0].wait()
    packed = dot(normed, wqf[...]).astype(BF16)
    queries = packed[:, :INNER]
    kv_cat[length:, :] = packed[:, INNER:]

    @pl.when(has_below & has_above)
    def _():
        pl.semaphore_wait(above, 1)

    @pl.when(has_below)
    def _():
        signal(above, me - GROUP)

    @pl.when(me > 0)
    def _():
        remote(tokens, prev, tok_s, tok_r, before).wait_recv()

    kv_cat[:length, :] = dot(normalize(prev[...]), wqf[:, INNER:]).astype(BF16)

    q_pos = iota((length, 2 * length), 0) + length
    k_pos = iota((length, 2 * length), 1)
    first_key = jnp.where(me == 0, length, 0)
    allowed = (k_pos <= q_pos) & (k_pos > q_pos - WINDOW) & (k_pos >= first_key)
    allowed = jnp.concatenate([allowed, allowed], axis=0)
    mixed = []
    for p in range(HEADS // 2):
        cols = slice(p * PAIR, (p + 1) * PAIR)
        scores = lax.dot_general(stack_heads(queries[:, cols]), kv_cat[:, cols], NT, preferred_element_type=F32)
        scores = jnp.where(allowed, scores, MASKED)
        highest = jnp.max(scores, axis=-1, keepdims=True)
        expsum = jnp.exp((scores - highest) * SCALE)
        total = jnp.sum(expsum, axis=-1, keepdims=True)
        values = kv_cat[:, INNER + p * PAIR:INNER + (p + 1) * PAIR]
        mixed.append(unstack_heads(dot(expsum.astype(BF16), values) / total).astype(BF16))
    weights[1].wait()
    stream = (tok.astype(F32) + dot(jnp.concatenate(mixed, axis=1), wof[...])).astype(BF16)

    slot = iota((capacity, length), 0)
    gather = onehot(slot == seg_lane[:capacity])
    edge_row = iota((TAIL, length), 0)
    edge_seg = jnp.where(edge_row == 0, starts - 1, jnp.where(edge_row == 1, -1, starts - 2))
    edge_gather = onehot((edge_row < 3) & (edge_seg == seg_lane[:TAIL]))
    edge_sum = dot(edge_gather, stream)
    edge_size = jnp.sum(edge_gather.astype(F32), axis=1, keepdims=True)
    for r in range(3):
        edges[lane, r, :, :width] = edge_sum[r:r + 1]
        edges[lane, r, :, width:] = jnp.broadcast_to(edge_size[r:r + 1], (1, 128))
    edge_copies = [
        remote(edges.at[lane], edges.at[lane], edge_s.at[k], edge_r.at[lane], group * GROUP + peer)
        for k, peer in enumerate(peers)
    ]
    down_copies = [
        remote(edges.at[lane], edges.at[GROUP], edge_s.at[GROUP + j], edge_r.at[GROUP], lax.rem(me + n - GROUP + j, n))
        for j in range(GROUP)
    ]
    up_copy = remote(edges.at[lane], edges.at[GROUP + 1], edge_s.at[GROUP - 1], edge_r.at[GROUP + 1], after)
    sends_down = (lane == 0) & (group > 0)
    sends_up = (lane == GROUP - 1) & (group < groups - 1)
    for copy in edge_copies:
        copy.start()

    @pl.when(sends_down)
    def _():
        for copy in down_copies:
            copy.start()

    @pl.when(sends_up)
    def _():
        up_copy.start()

    partial = dot(gather, stream)
    sizes = jnp.sum(gather.astype(F32), axis=1, keepdims=True)
    pooled = (partial / jnp.maximum(sizes, 1.0)).astype(BF16)
    weights[2].wait()

    short = dot(normalize(pooled), wqs[...]).astype(BF16)
    for j in range(GROUP):
        for part in range(3):
            parted[j, :, part * PAIR:(part + 1) * PAIR] = short[:, part * INNER + j * PAIR:part * INNER + (j + 1) * PAIR]
    part_copies = [
        remote(parted.at[peer], joined.at[lane], part_s.at[k], part_r.at[lane], group * GROUP + peer)
        for k, peer in enumerate(peers)
    ]
    for copy in part_copies:
        copy.start()
    joined[lane] = parted[lane]

    for k, peer in enumerate(peers):
        remote(marks.at[lane], marks.at[peer], marks_s.at[k], marks_r.at[peer], group * GROUP + peer).wait_recv()
    counts = [jnp.sum(marks[j][0:1], axis=1, keepdims=True) for j in range(GROUP)]
    firsts = [jnp.zeros_like(counts[0])]
    for j in range(GROUP - 1):
        firsts.append(firsts[-1] + counts[j])
    my_first = firsts[0]
    for j in range(1, GROUP):
        my_first = jnp.where(lane == j, firsts[j], my_first)

    place = iota((length, GROUP * capacity), 0)
    source = iota((length, GROUP * capacity), 1)
    owner_first = jnp.broadcast_to(firsts[0], place.shape)
    owner_count = jnp.broadcast_to(counts[0], place.shape)
    for j in range(1, GROUP):
        beyond = source >= j * capacity
        owner_first = jnp.where(beyond, firsts[j], owner_first)
        owner_count = jnp.where(beyond, counts[j], owner_count)
    within = source & (capacity - 1)
    compact = onehot((within < owner_count - 1) & (within + owner_first == place))

    for k, peer in enumerate(peers):
        remote(edges.at[lane], edges.at[peer], edge_s.at[k], edge_r.at[peer], group * GROUP + peer).wait_recv()

    @pl.when(group < groups - 1)
    def _():
        remote(edges.at[lane], edges.at[GROUP], edge_s.at[0], edge_r.at[GROUP], after).wait_recv()

    blank = jnp.zeros((TAIL - GROUP, width + 128), F32)
    closed = jnp.concatenate([edges[j, 0] for j in range(GROUP)] + [blank], axis=0)
    closed = closed + jnp.concatenate([edges[j + 1, 1] for j in range(GROUP)] + [blank], axis=0)
    closed = (closed[:, :width] / jnp.maximum(closed[:, width:width + 1], 1.0)).astype(BF16)
    closed = normalize(closed)
    closed_rows = jnp.concatenate(
        [
            dot(closed, wqs[:, pl.ds(pl.multiple_of(part * INNER + lane * PAIR, PAIR), PAIR)])
            for part in range(3)
        ],
        axis=1,
    ).astype(BF16)
    closed_id = iota((length, TAIL), 1)
    closed_place = jnp.full((length, TAIL), -1, jnp.int32)
    for j in range(GROUP):
        closed_place = jnp.where(closed_id == j, firsts[j] + counts[j] - 1, closed_place)
    closed_at = onehot(closed_place == iota((length, TAIL), 0))

    for k, peer in enumerate(peers):
        remote(parted.at[lane], joined.at[peer], part_s.at[k], part_r.at[peer], group * GROUP + peer).wait_recv()
    rows = (dot(compact, joined[...].reshape(GROUP * capacity, 3 * PAIR)) + dot(closed_at, closed_rows)).astype(BF16)
    kv_all[group] = rows[:, PAIR:]

    @pl.when(has_above & (group == 0))
    def _():
        pl.semaphore_wait(above, 1)

    def kv_copy(other):
        return remote(kv_all.at[group], kv_all.at[group], kv_s.at[other], kv_r.at[group], other * GROUP + lane)

    def send(step, carry):
        kv_copy(groups + group - step).start()
        return carry

    lax.fori_loop(group + 1, groups, send, 0)

    q_stack = stack_heads(rows[:, :PAIR])
    scores = lax.dot_general(q_stack, rows[:, PAIR:2 * PAIR], NT, preferred_element_type=F32)
    causal = i1 <= i0
    scores = jnp.where(jnp.concatenate([causal, causal], axis=0), scores, MASKED)
    row_max = jnp.max(scores, axis=-1, keepdims=True)
    expsum = jnp.exp((scores - row_max) * SCALE)
    row_total = jnp.sum(expsum, axis=-1, keepdims=True)
    running = dot(expsum.astype(BF16), rows[:, 2 * PAIR:])

    @pl.when((lane == 0) & (group > 0))
    def _():
        remote(edges.at[lane], edges.at[GROUP + 1], edge_s.at[0], edge_r.at[GROUP + 1], before).wait_recv()

    behind = jnp.where(lane == 0, GROUP + 1, lane - 1)
    last = edges[behind, 0] + edges[lane, 1]
    last_two = jnp.concatenate([last, edges[behind, 2], jnp.zeros((TAIL - 2, width + 128), F32)], axis=0)
    last_two = (last_two[:, :width] / jnp.maximum(last_two[:, width:width + 1], 1.0)).astype(BF16)
    lift = onehot(iota((length, capacity), 1) == seg_sub[:, :capacity] - 1)
    lift_tail = onehot(iota((length, TAIL), 1) == -seg_sub[:, :TAIL])
    pooled_lifted = dot(lift, pooled) + dot(lift_tail, last_two)

    def attend(step, carry):
        row_max, row_total, running = carry
        other = group - 1 - step
        remote(
            kv_all.at[other], kv_all.at[other], kv_s.at[other], kv_r.at[other], other * GROUP + lane
        ).wait_recv()
        block = kv_all[other]
        scores = lax.dot_general(q_stack, block[:, :PAIR], NT, preferred_element_type=F32)
        new_max = jnp.maximum(row_max, jnp.max(scores, axis=-1, keepdims=True))
        expsum = jnp.exp((scores - new_max) * SCALE)
        fading = jnp.exp((row_max - new_max) * SCALE)
        row_total = row_total * fading + jnp.sum(expsum, axis=-1, keepdims=True)
        running = running * fading + dot(expsum.astype(BF16), block[:, PAIR:])
        return new_max, row_total, running

    row_max, row_total, running = lax.fori_loop(0, group, attend, (row_max, row_total, running))
    mix[lane] = unstack_heads(running / row_total).astype(BF16)

    mix_copies = [
        remote(mix.at[lane], mix.at[lane], mix_s.at[k], mix_r.at[lane], group * GROUP + peer)
        for k, peer in enumerate(peers)
    ]
    for copy in mix_copies:
        copy.start()
    next_lead = lax.rem((group + 1) * GROUP, n)
    mt_copy = remote(
        mix.at[lane, pl.ds(length - TAIL, TAIL)], mix_tail.at[lane], mt_s, mt_r.at[lane], next_lead
    )

    @pl.when(group < groups - 1)
    def _():
        mt_copy.start()

    weights[3].wait()
    target = seg_sub + my_first - 1
    pick = onehot(i1 == target)
    pick_tail = onehot(iota((length, TAIL), 1) == target[:, :TAIL] + TAIL)
    for k, peer in enumerate(peers):
        remote(mix.at[peer], mix.at[peer], mix_s.at[k], mix_r.at[peer], group * GROUP + peer).wait_recv()

    @pl.when((lane == 0) & (group > 0))
    def _():
        for j in range(GROUP):
            remote(
                mix.at[j, pl.ds(length - TAIL, TAIL)], mix_tail.at[j], mt_s, mt_r.at[j], before
            ).wait_recv()

    mixed_rows = jnp.concatenate([mix[j] for j in range(GROUP)], axis=1)
    tail_rows = jnp.concatenate([mix_tail[j] for j in range(GROUP)], axis=1)
    lifted = (dot(pick, mixed_rows) + dot(pick_tail, tail_rows)).astype(BF16)
    short_out = (pooled_lifted + dot(lifted, wos[...])).astype(BF16)
    out[...] = (stream.astype(F32) + short_out.astype(F32)).astype(BF16)

    @pl.when(me < n - 1)
    def _():
        tok_copy.wait_send()

    @pl.when(sends_down)
    def _():
        for copy in down_copies:
            copy.wait_send()

    @pl.when(sends_up)
    def _():
        up_copy.wait_send()

    for copy in marks_copies + edge_copies + part_copies + mix_copies:
        copy.wait_send()

    def drain(other, carry):
        kv_copy(other).wait_send()
        return carry

    lax.fori_loop(group + 1, groups, drain, 0)

    @pl.when(group < groups - 1)
    def _():
        mt_copy.wait_send()


def shards(n, tokens, boundary, w_qkv_full, w_out_full, w_qkv_short, w_out_short):
    length, width = tokens.shape
    capacity = length // 2
    groups = n // GROUP
    vmem = pl.BlockSpec(memory_space=pltpu.VMEM)
    hbm = pl.BlockSpec(memory_space=pl.ANY)
    dma = pltpu.SemaphoreType.DMA
    return pl.pallas_call(
        functools.partial(kernel, n),
        out_shape=jax.ShapeDtypeStruct((length, width), BF16),
        in_specs=[hbm, hbm, hbm, hbm, hbm, hbm],
        out_specs=vmem,
        scratch_shapes=[
            pltpu.VMEM((length, width), BF16),
            pltpu.VMEM((1, length), jnp.int32),
            pltpu.VMEM(w_qkv_full.shape, BF16),
            pltpu.VMEM(w_out_full.shape, BF16),
            pltpu.VMEM(w_qkv_short.shape, BF16),
            pltpu.VMEM(w_out_short.shape, BF16),
            pltpu.VMEM((length, width), BF16),
            pltpu.VMEM((2 * length, 2 * INNER), BF16),
            pltpu.VMEM((GROUP + 2, 3, 1, width + 128), F32),
            pltpu.VMEM((GROUP, 8, length), jnp.int32),
            pltpu.VMEM((GROUP, capacity, 3 * PAIR), BF16),
            pltpu.VMEM((GROUP, capacity, 3 * PAIR), BF16),
            pltpu.VMEM((groups, length, 2 * PAIR), BF16),
            pltpu.VMEM((GROUP, length, PAIR), BF16),
            pltpu.VMEM((GROUP, TAIL, PAIR), BF16),
            pltpu.SemaphoreType.REGULAR,
            dma((6,)),
            dma, dma,
            dma((2 * GROUP,)), dma((GROUP + 2,)),
            dma((GROUP,)), dma((GROUP,)),
            dma((GROUP,)), dma((GROUP,)),
            dma((groups,)), dma((groups,)),
            dma((GROUP,)), dma((GROUP,)),
            dma, dma((GROUP,)),
        ],
        compiler_params=pltpu.CompilerParams(
            collective_id=0, has_side_effects=True, vmem_limit_bytes=54850 * 1024
        ),
    )(tokens, boundary.reshape(1, length), w_qkv_full, w_out_full, w_qkv_short, w_out_short)


def solution(mesh):
    return jax.shard_map(
        functools.partial(shards, mesh.shape["ctx"]),
        mesh=mesh,
        in_specs=(P(("parts", "ctx"), None), P(("parts", "ctx")), P(), P(), P(), P()),
        out_specs=P(("parts", "ctx"), None),
        check_vma=False,
    )
```
